256 devices in a mesh: ep: 64 (over x, z, y_hi), tp: 4 (over y_lo, core).
Axes of the slice: x: 4, y: 4 (y_hi: 2, y_lo: 2; y = y_hi * 2 + y_lo), z: 8, core: 2. Of those that a mesh axis runs over, the one named last changes fastest.
Arguments:
- tokens: bfloat16 [1024, 7168], P('ep', 'tp'), may hold values from -6 to 6
- expert_ids: int32 [1024, 8], P('ep'), may hold values from 0 to 63, all different within a row; in each aligned block of 16 rows (0 to 15, 16 to 31, ...) at most 4 rows name the same one
- gate_weights: float32 [1024, 8], P('ep'), may hold values from 0.1 to 1
- expert_gate_up: bfloat16 [64, 7168, 2, 1024], P('ep', None, None, 'tp'), may hold values from -0.0625 to 0.0625
- expert_down: bfloat16 [64, 7168, 1024], P('ep', None, 'tp'), may hold values from -0.1875 to 0.1875
- queries: bfloat16 [1024, 64, 576], P('ep', 'tp'), may hold values from -8 to 8
- latent_cache: bfloat16 [3072, 16, 576], P('ep'), may hold values from -8 to 8
- block_source: int32 [3072], replicated, may hold values from 0 to 3071, as said below
- block_request: int32 [3072], P('ep'), may hold values from -1 to 15, as said below
- block_used: int32 [3072], P('ep'), may hold values from 0 to 16, as said below
Outputs:
- moe_out: bfloat16 [1024, 7168], P('ep', 'tp')
- attention_out: bfloat16 [1024, 64, 512], P('ep', 'tp')
The draws below stay inside these ranges and needn't reach their ends.
Inputs may be any that keep to these rules, and one draw needn't show every extreme that they name: `expert_ids`: each row names 8 different experts; among the rows of one index of ep no expert is named by more than 4 rows, a bound that some block reaches. `block_source`: A permutation. `block_request`: within one index of ep each row holds a run of 1 to 3 consecutive slots, rows in order from the first slot, unused slots (-1) after them; some index of ep holds 3 slots for every row, and some has unused slots. `block_used`: 16 in every used slot but a row's last one, which holds 2 to 16; 0 in unused slots.
All inputs are finite; a program needn't handle non-finite values.
Results may differ from the reference program's by a relative error of at most 0.015.
Values may be sent and summed in bfloat16 or wider, within the bound.
A program may use at most 64 MiB of HBM per device.

```python
import math
import jax
import jax.numpy as jnp
import numpy as np
from jax import lax

D = 7168
FFE = 1024
HEADS = 64
KV = 512
TOPK = 8
BLK = 16
ROWS = 16
EXPERTS = 64
TOKENS = 1024
SLOTS = 48
ALL_SLOTS = 3072
CAP = 4
LAT = 576
FFE_PART = 256
N_EP = 64
N_TP = 4


def layout(key):
    subkeys = jax.random.split(jax.random.fold_in(key, 7), 5)
    devices = jnp.arange(N_EP, dtype=jnp.int32)
    device_caps = jax.random.randint(subkeys[0], (N_EP,), 0, 3)
    full_device = jax.random.randint(subkeys[1], (), 0, N_EP)
    light_device = (full_device + 1) % N_EP
    device_caps = jnp.where(devices == full_device, 2, jnp.where(devices == light_device, 0, device_caps))
    extra_blocks = jax.random.randint(subkeys[2], (N_EP, ROWS), 0, 3)
    counts = 1 + jnp.minimum(extra_blocks, device_caps[:, None])
    counts = jnp.where(devices[:, None] == full_device, 3, counts)
    run_ends = jnp.cumsum(counts, axis=1)
    starts = run_ends - counts
    slot_range = jnp.arange(SLOTS, dtype=jnp.int32)
    inside = (slot_range[None, :, None] >= starts[:, None, :]) & (slot_range[None, :, None] < run_ends[:, None, :])
    occupied = jnp.any(inside, axis=2)
    request = jnp.where(occupied, jnp.sum(inside * jnp.arange(ROWS, dtype=jnp.int32)[None, None, :], axis=2), -1)
    is_last = jnp.any(inside & (slot_range[None, :, None] == run_ends[:, None, :] - 1), axis=2)
    tail_used = jax.random.randint(subkeys[3], (N_EP, SLOTS), 2, BLK + 1)
    used_tokens = jnp.where(occupied, jnp.where(is_last, tail_used, BLK), 0)
    source = jax.random.permutation(subkeys[4], N_EP * SLOTS)
    return (request.reshape(-1), used_tokens.reshape(-1), source)


def draw_block_source(key, part):
    return layout(key)[2].astype(jnp.int32)


def draw_block_request(key, part):
    return layout(key)[0].astype(jnp.int32)


def draw_block_used(key, part):
    return layout(key)[1].astype(jnp.int32)


def draw_latent_cache(key, part):
    key = jax.random.fold_in(key, 11)
    cache_values = jnp.clip(jax.random.normal(key, (ALL_SLOTS, BLK, LAT), jnp.float32), -8.0, 8.0)
    return cache_values.astype(jnp.bfloat16)


def draw_queries(key, part):
    key = jax.random.fold_in(key, 13)
    query_values = jnp.clip(jax.random.normal(key, (TOKENS, HEADS, LAT), jnp.float32), -8.0, 8.0)
    return query_values.astype(jnp.bfloat16)


def block_levels(rng, extent, cuts, smallest, top_value):
    factor_of = 1.0
    for axis_at, blocks in cuts:
        draws = jax.random.uniform(jax.random.fold_in(jax.random.fold_in(rng, 6), axis_at), (blocks,), jnp.float32, smallest / len(cuts), top_value / len(cuts))
        factor_of = factor_of * jnp.repeat(jnp.exp(draws), extent[axis_at] // blocks).reshape((-1,) + (1,) * (len(extent) - 1 - axis_at))
    return factor_of


def routed_block(rng, own, number, rows, count, top, limit, slope):
    sequence = jax.random.permutation(rng, count)
    crowded, usual = portions_of(count, rows * top, limit, slope, True), portions_of(count, rows * top, limit, slope, False)
    places = jnp.arange(count)

    def named(lengths, turn):
        used = int((lengths > 0).sum())
        fixed = max(1, used // 4)
        moved = fixed + (places - fixed + turn * (used - fixed)) % max(1, count - fixed)
        return jnp.zeros((count,), jnp.int32).at[sequence[jnp.where(places < fixed, places, moved)]].set(jnp.asarray(lengths, jnp.int32))

    lengths = jnp.where(number % 4 == 0, named(crowded, number // 4), named(usual, number - number // 4 - 1))
    mixed = jax.random.permutation(jax.random.fold_in(own, 3), count)
    donor, taker = mixed[0:count // 2 * 2:2], mixed[1:count // 2 * 2:2]
    margin = jnp.minimum(lengths[donor] - 1, limit - lengths[taker]) // 2
    margin = jnp.where((donor == sequence[0]) | (taker == sequence[0]) | (lengths[taker] == 0), 0, jnp.maximum(margin, 0))
    moved = jax.random.randint(jax.random.fold_in(own, 4), (count // 2,), 0, 1 << 20) % (margin + 1)
    lengths = lengths.at[donor].add(-moved).at[taker].add(moved)
    members = jnp.searchsorted(jnp.cumsum(lengths), jnp.arange(rows * top), side="right").astype(jnp.int32)
    grid = members.reshape(top, rows).T
    grid = grid[jax.random.permutation(jax.random.fold_in(own, 1), rows)]
    turn = jax.random.randint(jax.random.fold_in(own, 2), (rows, 1), 0, top)
    return jnp.take_along_axis(grid, (jnp.arange(top)[None, :] + turn) % top, axis=1)


def portions_of(amount, total, limit, skew, full):
    portions = [(1 << 20) // math.isqrt(rank ** skew) + 1 for rank in range(1, amount + 1)]
    largest = limit if full else min(limit, max(-(-total // amount), total * portions[0] // sum(portions)))
    least = 1 if total - largest >= amount - 1 else 0
    holding, rest = [largest] + [least] * (amount - 1), total - largest - least * (amount - 1)
    while rest > 0:
        candidates = [i for i in range(1, amount) if holding[i] < largest] or [i for i in range(1, amount) if holding[i] < limit]
        pool, budget = sum([portions[i] for i in candidates]), rest
        for i in candidates:
            more = min(limit - holding[i], max(1, budget * portions[i] // pool), rest)
            holding[i] = holding[i] + more
            rest = rest - more
    return np.array(holding)


def noise(own_key, shape, scale, bound, cuts=(), kind=jnp.bfloat16):
    entries = jax.random.normal(own_key, shape, jnp.float32) * scale
    if len(cuts) > 0:
        entries = block_levels(own_key, shape, cuts, -0.22, 0.18) * entries
    return jnp.clip(entries, min=-bound, max=bound).astype(kind)


def setup_inputs(seed: int = 0) -> dict:
    seeds = jax.random.split(jax.random.key(seed), 11)
    tokens = noise(seeds[0], (TOKENS, D), 1.0, 6.0, ((0, 64), (1, 4)))
    expert_ids_keys = jax.random.split(jax.random.fold_in(seeds[1], 1), TOKENS // ROWS)
    expert_ids_turns = jax.random.permutation(jax.random.fold_in(seeds[1], 3), TOKENS // ROWS)
    expert_ids = jax.vmap(lambda own, number: routed_block(jax.random.fold_in(seeds[1], 2), own, number, ROWS, EXPERTS, TOPK, CAP, 2))(expert_ids_keys, expert_ids_turns).reshape((TOKENS, TOPK))
    gate_weights = jnp.clip(0.1 + 0.9 * jax.random.uniform(seeds[2], (TOKENS, TOPK), jnp.float32) ** block_levels(seeds[2], (TOKENS, TOPK), ((0, 64),), -0.2, 0.2), 0.1, 1.0)
    expert_gate_up = noise(seeds[3], (EXPERTS, D, 2, FFE), D ** -0.5, 0.0625, ((0, 64), (3, 4)))
    expert_down = noise(seeds[4], (EXPERTS, D, FFE), FFE ** -0.5, 0.1875, ((0, 64), (2, 4)))
    queries = draw_queries(jax.random.fold_in(seeds[10], 71), 0)
    latent_cache = draw_latent_cache(jax.random.fold_in(seeds[10], 71), 0)
    block_source = draw_block_source(jax.random.fold_in(seeds[10], 71), 0)
    block_request = draw_block_request(jax.random.fold_in(seeds[10], 71), 0)
    block_used = draw_block_used(jax.random.fold_in(seeds[10], 71), 0)
    return dict(tokens=tokens, expert_ids=expert_ids, gate_weights=gate_weights, expert_gate_up=expert_gate_up, expert_down=expert_down, queries=queries, latent_cache=latent_cache, block_source=block_source, block_request=block_request, block_used=block_used)


score_scale = 192.0 ** -0.5


def expert_layer(tokens, expert_ids, gate_weights, expert_gate_up, expert_down):
    pair_count = ROWS * TOPK
    flat_ids = expert_ids.reshape(N_EP, pair_count).astype(jnp.int32)
    expert_hot = (flat_ids[:, :, None] == jnp.arange(EXPERTS, dtype=jnp.int32)[None, None, :]).astype(jnp.int32)
    earlier = jnp.sum((jnp.cumsum(expert_hot, axis=1) - expert_hot) * expert_hot, axis=2).astype(jnp.int32)
    device_index = jnp.broadcast_to(jnp.arange(N_EP, dtype=jnp.int32)[:, None], (N_EP, pair_count))
    row_index = jnp.broadcast_to((jnp.arange(pair_count, dtype=jnp.int32) // TOPK)[None, :], (N_EP, pair_count))
    token_index = device_index * ROWS + row_index
    slot_table = jnp.full((EXPERTS, N_EP, CAP), -1, jnp.int32).at[flat_ids, device_index, earlier].set(token_index)
    weight_table = jnp.zeros((EXPERTS, N_EP, CAP), jnp.float32).at[flat_ids, device_index, earlier].set(
        gate_weights.reshape(N_EP, pair_count).astype(jnp.float32))

    def one_expert(running, expert):
        token_slots = slot_table[expert].reshape(-1)
        present = token_slots >= 0
        safe_index = jnp.maximum(token_slots, 0).astype(jnp.int32)
        picked = jnp.where(present[:, None], tokens[safe_index], jnp.zeros((), tokens.dtype))
        expert_block = lax.dynamic_index_in_dim(expert_gate_up, expert.astype(jnp.int32), 0, keepdims=False)
        gate_and_up = jnp.einsum("rd,dgf->rgf", picked.astype(jnp.float32), expert_block.astype(jnp.float32))
        hidden = (jax.nn.silu(gate_and_up[:, 0]) * gate_and_up[:, 1]).astype(jnp.bfloat16)
        hidden = lax.optimization_barrier(hidden)
        down_block = lax.dynamic_index_in_dim(expert_down, expert.astype(jnp.int32), 0, keepdims=False).astype(jnp.float32)
        groups = hidden.astype(jnp.float32).reshape(-1, N_TP, FFE_PART)
        partial_value = jnp.einsum("rpf,dpf->prd", groups, down_block.reshape(D, N_TP, FFE_PART)).astype(jnp.bfloat16)
        partial_value = lax.optimization_barrier(partial_value)
        summed = jnp.sum(partial_value.astype(jnp.float32), axis=0).astype(jnp.bfloat16)
        summed = lax.optimization_barrier(summed)
        weighted = summed.astype(jnp.float32) * weight_table[expert].reshape(-1)[:, None]
        weighted = jnp.where(present[:, None], weighted, jnp.zeros((), jnp.float32))
        return running.at[safe_index].add(weighted), None

    start = jnp.zeros((TOKENS, D), jnp.float32)
    result, unused = lax.scan(one_expert, start, jnp.arange(EXPERTS, dtype=jnp.int32))
    return result.astype(jnp.bfloat16)


def attention_layer(queries, latent_cache, block_source, block_request, block_used):
    moved_cache = latent_cache[block_source.astype(jnp.int32)].reshape(N_EP, SLOTS * BLK, LAT)
    owners = jnp.repeat(block_request.reshape(N_EP, SLOTS), BLK, axis=1)
    limits = jnp.repeat(block_used.reshape(N_EP, SLOTS), BLK, axis=1)
    within = jnp.tile(jnp.arange(BLK, dtype=jnp.int32), SLOTS)
    grouped = queries.reshape(N_EP, ROWS, HEADS, LAT)

    def one_device(device_inputs):
        query_block, key_block, owner_row, limit_row = device_inputs
        visible = (owner_row[None, :] == jnp.arange(ROWS, dtype=jnp.int32)[:, None]) & (within < limit_row)[None, :]
        scores = jnp.einsum("rhc,tc->rht", query_block.astype(jnp.float32), key_block.astype(jnp.float32)) * score_scale
        scores = jnp.where(visible[:, None, :], scores, -jnp.inf)
        row_max = jnp.max(scores, axis=2, keepdims=True)
        exponent_terms = jnp.exp(scores - row_max)
        weights = (exponent_terms / jnp.sum(exponent_terms, axis=2, keepdims=True)).astype(jnp.bfloat16)
        weights = lax.optimization_barrier(weights)
        attended = jnp.einsum("rht,tc->rhc", weights.astype(jnp.float32), key_block[:, :KV].astype(jnp.float32))
        return attended.astype(jnp.bfloat16)

    result = lax.map(one_device, (grouped, moved_cache, owners, limits))
    return result.reshape(TOKENS, HEADS, KV)


def reference(tokens, expert_ids, gate_weights, expert_gate_up, expert_down, queries, latent_cache, block_source, block_request, block_used):
    moe_out = expert_layer(tokens, expert_ids, gate_weights, expert_gate_up, expert_down)
    attention_out = attention_layer(queries, latent_cache, block_source, block_request, block_used)
    return (moe_out, attention_out)
```

```python
import jax
import jax.numpy as jnp
from jax import lax
from jax.experimental import pallas as pl
from jax.experimental.pallas import tpu as pltpu
from jax.sharding import PartitionSpec as P

MESH = pl.DeviceIdType.MESH

D = 7168
QF = 1792
HID = 256
ROWS = 16
NX, NZ = 4, 8
CAP = 4
SLOTS = 48
BLK = 16
LAT = 576
KV = 512
PART = 384
KL = 2 * PART
ORDER = (0, 1, 3, 2)

score_scale = 192.0 ** (-0.5)


def place():
    ep, tp = lax.axis_index("ep"), lax.axis_index("tp")
    x = lax.div(ep, 16)
    z = lax.rem(lax.div(ep, 2), NZ)
    return x, z, lax.rem(ep, 2), lax.div(tp, 2), lax.rem(tp, 2)


def device(x, z, yh, yl, c):
    return ((x * NZ + z) * 2 + yh, yl * 2 + c)


class Copies:
    def __init__(self, send, recv):
        self.send, self.recv, self.made, self.count = send, recv, {}, 0

    def start(self, name, src, dst, to):
        i = self.count
        self.count += 1
        copy = pltpu.make_async_remote_copy(
            src_ref=src,
            dst_ref=dst,
            send_sem=self.send.at[i],
            recv_sem=self.recv.at[i],
            device_id=to,
            device_id_type=MESH,
        )
        copy.start()
        self.made[name] = copy

    def arrived(self, name):
        self.made[name].wait_recv()

    def finish(self):
        for copy in self.made.values():
            copy.wait_send()


def kernel(
    meta_ref,
    tok_ref,
    cq_ref,
    jb_ref,
    q_ref,
    mask_ref,
    wgu_ref,
    wd_ref,
    moe_ref,
    att_ref,
    send_sem,
    recv_sem,
    local_sem,
    wgu,
    wd,
    metag,
    meta_t,
    rows,
    selw,
    xsend,
    slots,
    other,
    part,
    mate,
    chip,
    back,
    ebuf,
    bbuf,
    zsend,
    zrecv,
    cz,
    cxs,
    cxr,
    cm,
    keys,
    qp,
):
    x, z, yh, yl, c = place()
    tp = yl * 2 + c
    group = lax.rem(yl + yh, 2)
    copies = Copies(send_sem, recv_sem)

    def at_x(e):
        return device(lax.rem(x + e, NX), z, yh, yl, c)

    def at_z(d):
        return device(x, lax.rem(z + d, NZ), yh, yl, c)

    core = device(x, z, yh, yl, 1 - c)
    near = device(x, z, yh, 1 - yl, c)
    cross = device(x, z, 1 - yh, 1 - yl, c)
    far = device(x, z, 1 - yh, yl, c)

    wgu_copy = pltpu.make_async_copy(wgu_ref, wgu, local_sem.at[0])
    wd_copy = pltpu.make_async_copy(wd_ref, wd, local_sem.at[1])
    wgu_copy.start()
    wd_copy.start()

    barrier = pltpu.get_barrier_semaphore()
    partners = [at_x(e) for e in range(1, NX)] + [at_z(d) for d in range(1, NZ)]
    partners += [core, near, cross, far]
    for partner in partners:
        pl.semaphore_signal(barrier, inc=1, device_id=partner, device_id_type=MESH)
    pl.semaphore_wait(barrier, len(partners))

    far_first = (1, 7, 2, 6, 3, 5, 4)
    for d in far_first:
        copies.start(("meta", d), meta_ref, metag.at[d], at_z(d))
    for d in far_first:
        copies.start(("tok", d), tok_ref, rows.at[pl.ds(d * ROWS, ROWS)], at_z(d))

    def piece(d):
        to = lax.rem(z + d, NZ)
        lane = pl.multiple_of(lax.rem(to, 2) * 256, 256)
        return cq_ref.at[lax.div(to, 2), :, pl.ds(lane, PART)]

    own_piece = pltpu.make_async_copy(piece(0), cz.at[pl.ds(0, SLOTS)], local_sem.at[2])
    own_piece.start()
    for d in far_first:
        copies.start(("cz", d), piece(d), cz.at[pl.ds(d * SLOTS, SLOTS)], at_z(d))

    metag[0] = meta_ref[...]
    rows[0:ROWS] = tok_ref[...]
    for d in far_first:
        copies.arrived(("meta", d))
    meta_t[...] = metag[...].reshape(NZ * ROWS, 128).T

    slot_at = lax.broadcasted_iota(jnp.int32, (32, 128), 0)
    row_at = lax.broadcasted_iota(jnp.int32, (32, 128), 1)
    same_source = lax.shift_right_logical(slot_at, 2) == lax.shift_right_logical(row_at, 4)
    slot_rank = lax.bitwise_and(slot_at, 3).astype(jnp.float32)

    def chosen(e, rel):
        at = z * 8 + lax.rem(x + e, NX) * 2 + (yh if rel == 0 else 1 - yh)
        code = meta_t[pl.ds(at, 1), :]
        weight = meta_t[pl.ds(at + 64, 1), :]
        hot = same_source & (slot_rank == code)
        selw[pl.ds(e * 64 + rel * 32, 32), :] = jnp.where(hot, weight, 0.0)
        return jnp.where(hot, 1.0, 0.0).astype(jnp.bfloat16)

    picks = {}
    for e in ORDER:
        picks[e] = jnp.concatenate([chosen(e, 0), chosen(e, 1)], axis=0)
    for d in far_first:
        copies.arrived(("tok", d))

    def own_rows(e):
        return pl.ds(e * 64, 32)

    def other_rows(e):
        return pl.ds(e * 64 + 32, 32)

    def pick(e):
        return jnp.dot(picks[e], rows[...], preferred_element_type=jnp.float32).astype(jnp.bfloat16)

    def along_y(e):
        copies.start(("near", e), slots.at[tp, own_rows(e)], slots.at[tp, own_rows(e)], near)
        copies.start(("cross", e), other.at[e], slots.at[tp, other_rows(e)], cross)
        copies.start(("far", e), other.at[e], slots.at[tp, other_rows(e)], far)

    picked = pick(0)
    slots[tp, 0:32] = picked[:32]
    other[0] = picked[32:]
    along_y(0)
    for e in (1, 3, 2):
        xsend[e] = pick(e)
        copies.start(("x0", e), xsend.at[e, pl.ds(0, 32)], slots.at[tp, own_rows(e)], at_x(e))
        copies.start(("x1", e), xsend.at[e, pl.ds(32, 32)], other.at[e], at_x(e))

    def from_x(e):
        copies.arrived(("x0", e))
        copies.arrived(("x1", e))
        along_y(e)

    near_tp = (1 - yl) * 2 + c

    def to_core(e):
        whole = pl.ds(e * 64, 64)
        copies.arrived(("near", e))
        copies.arrived(("cross", e))
        copies.start(("core_n", e), slots.at[near_tp, whole], slots.at[near_tp, whole], core)
        copies.arrived(("far", e))
        copies.start(("core_o", e), slots.at[tp, whole], slots.at[tp, whole], core)

    def expert(e):
        copies.arrived(("core_n", e))
        copies.arrived(("core_o", e))

        def add(k, total):
            at = pl.multiple_of(k * QF, 256)
            return total + jnp.dot(
                slots[k, pl.ds(e * 64, 64), :],
                wgu[pl.ds(at, QF), :],
                preferred_element_type=jnp.float32,
            )

        both = lax.fori_loop(0, 4, add, jnp.zeros((64, 2 * HID), jnp.float32))
        gate, up = both[:, :HID], both[:, HID:]
        hidden = (gate / (1.0 + jnp.exp(-gate)) * up).astype(jnp.bfloat16)

        @pl.loop(0, 4)
        def down(k):
            at = pl.multiple_of(k * QF, 256)
            part[e, lax.rem(k, 2), lax.div(k, 2)] = lax.dot_general(
                hidden,
                wd[pl.ds(at, QF), :],
                (((1,), (1,)), ((), ())),
                preferred_element_type=jnp.float32,
            ).astype(jnp.bfloat16)

        copies.start(("mate", e), part.at[e, 1 - c], mate.at[e], core)

    def chip_sum(e):
        copies.arrived(("mate", e))
        for h in range(2):
            chip[e, h] = (
                part[e, c, h].astype(jnp.float32) + mate[e, h].astype(jnp.float32)
            ).astype(jnp.bfloat16)
        low, high = pl.ds(0, 32), pl.ds(32, 32)
        copies.start(("r_near", e), chip.at[e, 1 - yl, low], back.at[e, 0], near)
        copies.start(("r_cross", e), chip.at[e, 1 - yl, high], back.at[e, 1], cross)
        copies.start(("r_far", e), chip.at[e, yl, high], back.at[e, 2], far)

    def expert_out(e):
        into = bbuf if e == 0 else ebuf
        copies.arrived(("r_near", e))
        into[e, 0:32] = (
            chip[e, yl, 0:32].astype(jnp.float32) + back[e, 0].astype(jnp.float32)
        ).astype(jnp.bfloat16)
        copies.arrived(("r_cross", e))
        copies.arrived(("r_far", e))
        into[e, 32:64] = (
            back[e, 1].astype(jnp.float32) + back[e, 2].astype(jnp.float32)
        ).astype(jnp.bfloat16)
        if e != 0:
            copies.start(("r_x", e), ebuf.at[e], bbuf.at[e], at_x(NX - e))

    def cache_swap():
        own_piece.wait()
        for d in far_first:
            copies.arrived(("cz", d))
        half = NZ * SLOTS
        copies.start(("swap", 0), cz.at[pl.ds(0, half)], cz.at[pl.ds(half, half)], cross)

    def cache_pick():
        copies.arrived(("swap", 0))
        lanes = lax.broadcasted_iota(jnp.int32, (NZ * SLOTS, 128), 1)
        for e in (2, 1, 3, 0):
            at = pl.multiple_of(lax.rem(x + e, NX) * (NZ * SLOTS), 128)
            wanted = jb_ref[pl.ds(at, NZ * SLOTS), :]
            hot = jnp.concatenate(
                [
                    jnp.where(wanted == lanes + 128 * k, 1.0, 0.0).astype(jnp.bfloat16)
                    for k in range(6)
                ],
                axis=1,
            )
            found = jnp.dot(hot, cz[...], preferred_element_type=jnp.float32).astype(jnp.bfloat16)
            if e == 0:
                cxr[0] = found
            else:
                cxs[e] = found
                copies.start(("cx", e), cxs.at[e], cxr.at[e], at_x(e))

    local = {}

    def cache_merge():
        for e in (1, 3, 2):
            copies.arrived(("cx", e))
        cm[...] = (cxr[0] + cxr[1]) + (cxr[2] + cxr[3])
        lane = pl.multiple_of(lax.rem(z, 2) * PART, 128)
        landing = keys.at[group, c, lax.div(z, 2), :, pl.ds(lane, PART)]

        def of(d):
            at = pl.multiple_of(lax.rem(z + d, NZ) * SLOTS, 16)
            return cm.at[pl.ds(at, SLOTS)]

        local["k"] = pltpu.make_async_copy(of(0), landing, local_sem.at[3])
        local["k"].start()
        for d in far_first:
            copies.start(("k", d), of(d), landing, at_z(d))

    def cache_tp():
        local["k"].wait()
        for d in far_first:
            copies.arrived(("k", d))
        copies.start(("k_near", 0), keys.at[group, c], keys.at[group, c], near)
        copies.start(("k_core", 0), keys.at[group, c], keys.at[group, c], core)

    def cache_core():
        copies.arrived(("k_near", 0))
        copies.start(("k_core", 1), keys.at[1 - group, c], keys.at[1 - group, c], core)

    def attention():
        copies.arrived(("k_core", 0))
        copies.arrived(("k_core", 1))
        qp[...] = jnp.zeros_like(qp)
        qp[:, 0:256] = q_ref[:, 0:256]
        qp[:, PART : PART + LAT - 256] = q_ref[:, 256:LAT]
        held = keys[...].reshape(SLOTS * BLK, KL)
        scores = (
            lax.dot_general(
                qp[...], held, (((1,), (1,)), ((), ())), preferred_element_type=jnp.float32
            )
            * score_scale
        )
        seen = jnp.broadcast_to(mask_ref[...][:, None, :], (ROWS, 16, SLOTS * BLK)).reshape(
            256, SLOTS * BLK
        )
        scores = jnp.where(seen > 0.0, scores, -1e30)
        terms = jnp.exp(scores - jnp.max(scores, axis=1, keepdims=True))
        weights = (terms / jnp.sum(terms, axis=1, keepdims=True)).astype(jnp.bfloat16)
        att_ref[:, 0:256] = jnp.dot(
            weights, held[:, 0:256], preferred_element_type=jnp.float32
        ).astype(jnp.bfloat16)
        att_ref[:, 256:KV] = jnp.dot(
            weights, held[:, PART : PART + 256], preferred_element_type=jnp.float32
        ).astype(jnp.bfloat16)

    cache_swap()
    from_x(1)
    to_core(0)
    wgu_copy.wait()
    wd_copy.wait()
    expert(0)
    from_x(3)
    to_core(1)
    cache_pick()
    from_x(2)
    chip_sum(0)
    expert(1)
    to_core(3)
    chip_sum(1)
    expert(3)
    cache_merge()
    to_core(2)
    chip_sum(3)
    expert_out(0)
    expert(2)
    expert_out(1)
    cache_tp()
    chip_sum(2)
    expert_out(3)
    cache_core()
    expert_out(2)
    attention()

    for e in (1, 3, 2):
        copies.arrived(("r_x", e))
    wide = selw[...]
    high = wide.astype(jnp.bfloat16)
    low = (wide - high.astype(jnp.float32)).astype(jnp.bfloat16)
    joined = bbuf[...].reshape(NX * 64, QF)
    contract = (((0,), (0,)), ((), ()))
    summed = lax.dot_general(high, joined, contract, preferred_element_type=jnp.float32)
    summed += lax.dot_general(low, joined, contract, preferred_element_type=jnp.float32)
    zsend[...] = summed.astype(jnp.bfloat16)
    for d in far_first:
        copies.start(("z", d), zsend.at[pl.ds(d * ROWS, ROWS)], zrecv.at[d], at_z(NZ - d))
    total = summed[0:ROWS]
    for d in far_first:
        copies.arrived(("z", d))
        total += zrecv[d].astype(jnp.float32)
    moe_ref[...] = total.astype(jnp.bfloat16)
    copies.finish()


def routing(expert_ids, gate_weights):
    hot = expert_ids[:, :, None] == jnp.arange(64, dtype=jnp.int32)[None, None, :]
    named = jnp.any(hot, axis=1)
    weight = jnp.sum(jnp.where(hot, gate_weights[:, :, None], 0.0), axis=1)
    named_f = named.astype(jnp.float32)
    earlier = jnp.tril(jnp.ones((ROWS, ROWS), jnp.float32), -1)
    rank = jnp.sum(earlier[:, :, None] * named_f[None, :, :], axis=1)
    code = jnp.where(named, rank, -1.0)

    def by_plane(v):
        return v.reshape(ROWS, NX, NZ, 2).transpose(0, 2, 1, 3).reshape(ROWS, 64)

    return jnp.concatenate([by_plane(code), by_plane(weight)], axis=1)


def body(
    tokens,
    expert_ids,
    gate_weights,
    expert_gate_up,
    expert_down,
    queries,
    latent_cache,
    block_source,
    block_request,
    block_used,
):
    x, z, yh, yl, c = place()
    group = lax.rem(yl + yh, 2) * 2 + c
    meta = routing(expert_ids, gate_weights)

    pieces = lax.dynamic_slice_in_dim(latent_cache, group * 4, 4, axis=1)
    pieces = jnp.pad(pieces.transpose(1, 0, 2), ((0, 0), (0, 0), (0, 640 - LAT)))

    wanted = lax.dynamic_index_in_dim(
        block_source.reshape(NX, NZ, 2, SLOTS), yh, axis=2, keepdims=False
    ).reshape(-1)
    owner = wanted // SLOTS
    place_of = (
        ((owner + yh) % 2) * NZ + (z + NZ - (owner // 2) % NZ) % NZ
    ) * SLOTS + wanted % SLOTS
    place_of = jnp.where(owner // 16 == x, place_of, -1)
    place_of = jnp.broadcast_to(place_of[:, None], (NX * NZ * SLOTS, 128))

    mine = block_request[None, :] == jnp.arange(ROWS, dtype=jnp.int32)[:, None]
    within = jnp.arange(BLK, dtype=jnp.int32)[:, None] < block_used[None, :]
    mask = (mine[:, None, :] & within[None, :, :]).astype(jnp.float32)
    mask = mask.reshape(ROWS, BLK * SLOTS)

    gate_up = expert_gate_up[0].reshape(D, 2 * HID)

    bf16, f32 = jnp.bfloat16, jnp.float32
    vmem = pl.BlockSpec(memory_space=pltpu.VMEM)
    anyspace = pl.BlockSpec(memory_space=pl.ANY)
    count = 96
    moe, attended = pl.pallas_call(
        kernel,
        out_shape=(
            jax.ShapeDtypeStruct((ROWS, QF), bf16),
            jax.ShapeDtypeStruct((256, KV), bf16),
        ),
        in_specs=[vmem] * 6 + [anyspace] * 2,
        out_specs=(vmem, vmem),
        scratch_shapes=[
            pltpu.SemaphoreType.DMA((count,)),
            pltpu.SemaphoreType.DMA((count,)),
            pltpu.SemaphoreType.DMA((4,)),
            pltpu.VMEM((D, 2 * HID), bf16),
            pltpu.VMEM((D, HID), bf16),
            pltpu.VMEM((NZ, ROWS, 128), f32),
            pltpu.VMEM((128, 128), f32),
            pltpu.VMEM((NZ * ROWS, QF), bf16),
            pltpu.VMEM((256, 128), f32),
            pltpu.VMEM((NX, 64, QF), bf16),
            pltpu.VMEM((4, 256, QF), bf16),
            pltpu.VMEM((NX, 32, QF), bf16),
            pltpu.VMEM((NX, 2, 2, 64, QF), bf16),
            pltpu.VMEM((NX, 2, 64, QF), bf16),
            pltpu.VMEM((NX, 2, 64, QF), bf16),
            pltpu.VMEM((NX, 3, 32, QF), bf16),
            pltpu.VMEM((NX, 64, QF), bf16),
            pltpu.VMEM((NX, 64, QF), bf16),
            pltpu.VMEM((NZ * ROWS, QF), bf16),
            pltpu.VMEM((NZ, ROWS, QF), bf16),
            pltpu.VMEM((2 * NZ * SLOTS, PART), bf16),
            pltpu.VMEM((NX, NZ * SLOTS, PART), bf16),
            pltpu.VMEM((NX, NZ * SLOTS, PART), bf16),
            pltpu.VMEM((NZ * SLOTS, PART), bf16),
            pltpu.VMEM((2, 2, 4, SLOTS, KL), bf16),
            pltpu.VMEM((256, KL), bf16),
        ],
        compiler_params=pltpu.CompilerParams(
            collective_id=0, has_side_effects=True, vmem_limit_bytes=56 * 2**20
        ),
        cost_estimate=pl.CostEstimate(
            flops=4 * 10**9, bytes_accessed=13 * 10**6, transcendentals=3 * 10**5
        ),
        name="layer",
    )(
        meta,
        tokens,
        pieces,
        place_of,
        queries.reshape(256, LAT),
        mask,
        gate_up,
        expert_down[0],
    )
    return moe, attended.reshape(ROWS, 16, KV)


def solution(mesh):
    placed = (
        P("ep", "tp"),
        P("ep", None),
        P("ep", None),
        P("ep", None, None, "tp"),
        P("ep", None, "tp"),
        P("ep", "tp", None),
        P("ep", None, None),
        P(),
        P("ep"),
        P("ep"),
    )
    return jax.shard_map(
        body,
        mesh=mesh,
        in_specs=placed,
        out_specs=(P("ep", "tp"), P("ep", "tp", None)),
        check_vma=False,
    )
```

```python
import jax
import jax.numpy as jnp
from jax import lax
from jax.experimental import pallas as pl
from jax.experimental.pallas import tpu as pltpu
from jax.sharding import PartitionSpec as P

MESH = pl.DeviceIdType.MESH

D = 7168
QF = 1792
HID = 256
ROWS = 16
NX, NZ = 4, 8
SLOTS = 48
HALF = NZ * SLOTS
BLK = 16
LAT = 576
KV = 512
PIECES = 3
KL = 2 * PIECES * 128
TOK = SLOTS * BLK
OFFSETS = (0, 1, 3, 2)
ALONG_Z = (4, 3, 5, 2, 6, 1, 7)
WIDTHS = (384, 640, 768)
STARTS = (0, 384, 1024)
CHUNK = 256

score_scale = 192.0 ** (-0.5)


def place():
    ep, tp = lax.axis_index("ep"), lax.axis_index("tp")
    x = lax.div(ep, 16)
    z = lax.rem(lax.div(ep, 2), NZ)
    return x, z, lax.rem(ep, 2), lax.div(tp, 2), lax.rem(tp, 2)


def device(x, z, yh, yl, c):
    return ((x * NZ + z) * 2 + yh, yl * 2 + c)


def iota(shape, axis):
    return lax.broadcasted_iota(jnp.int32, shape, axis)


def one_hot(equal):
    return jnp.where(equal, 1.0, 0.0).astype(jnp.bfloat16)


def over(values, divisor):
    return jnp.floor((values + 0.5) * (1.0 / divisor))


def dot(a, b):
    return jnp.dot(a, b, preferred_element_type=jnp.float32)


class Copies:
    def __init__(self, send, recv):
        self.send, self.recv, self.made, self.count = send, recv, {}, 0

    def start(self, name, src, dst, to):
        i = self.count
        self.count += 1
        copy = pltpu.make_async_remote_copy(
            src_ref=src,
            dst_ref=dst,
            send_sem=self.send.at[i],
            recv_sem=self.recv.at[i],
            device_id=to,
            device_id_type=MESH,
        )
        copy.start()
        self.made[name] = copy

    def arrived(self, name):
        self.made[name].wait_recv()

    def finish(self):
        for copy in self.made.values():
            copy.wait_send()


def kernel(
    ids_ref,
    gate_ref,
    tok_ref,
    cache_ref,
    source_ref,
    q_ref,
    request_ref,
    used_ref,
    wgu_ref,
    wd_ref,
    moe_ref,
    att_ref,
    send_sem,
    recv_sem,
    local_sem,
    raw,
    wgu,
    wd,
    perm,
    meta,
    metag,
    rows,
    pick,
    selw,
    xsend,
    slots,
    other,
    both,
    hidden,
    part,
    mate,
    chip,
    back,
    ebuf,
    bbuf,
    zsend,
    zrecv,
    cq,
    pos,
    jb,
    cz,
    hots,
    cxs,
    cxr,
    cm,
    keys,
    qp,
):
    x, z, yh, yl, c = place()
    tp = yl * 2 + c
    near_tp = (1 - yl) * 2 + c
    group = lax.rem(yl + yh, 2)
    copies = Copies(send_sem, recv_sem)

    def at_x(e):
        return device(lax.rem(x + e, NX), z, yh, yl, c)

    def at_z(d):
        return device(x, lax.rem(z + d, NZ), yh, yl, c)

    core = device(x, z, yh, yl, 1 - c)
    near = device(x, z, yh, 1 - yl, c)
    cross = device(x, z, 1 - yh, 1 - yl, c)
    far = device(x, z, 1 - yh, yl, c)

    barrier = pltpu.get_barrier_semaphore()
    partners = [at_x(e) for e in range(1, NX)] + [at_z(d) for d in range(1, NZ)]
    partners += [core, near, cross, far]
    for partner in partners:
        pl.semaphore_signal(barrier, inc=1, device_id=partner, device_id_type=MESH)

    raw_copy = pltpu.make_async_copy(wgu_ref, raw, local_sem.at[0])
    wd_copy = pltpu.make_async_copy(wd_ref, wd, local_sem.at[1])
    raw_copy.start()
    wd_copy.start()

    meta[...] = jnp.zeros_like(meta)
    meta[0:8, 0:ROWS] = ids_ref[...].astype(jnp.float32)
    meta[8:16, 0:ROWS] = gate_ref[...]
    to_lanes = jnp.where(iota((128, 128), 1) == iota((128, 128), 0) + z * ROWS, 1.0, 0.0)
    meta[...] = jnp.dot(
        meta[...],
        to_lanes,
        precision=lax.Precision.HIGHEST,
        preferred_element_type=jnp.float32,
    )
    metag[0] = meta[...]
    own_z = pl.ds(pl.multiple_of(z * ROWS, ROWS), ROWS)
    rows[own_z, :] = tok_ref[...]
    pl.semaphore_wait(barrier, len(partners))

    def lanes(f):
        return pl.ds(STARTS[f], WIDTHS[f])

    def send_tables():
        for d in ALONG_Z:
            copies.start(("meta", d), meta, metag.at[d], at_z(d))

    def send_rows(f):
        for d in ALONG_Z:
            copies.start(
                ("tok", f, d), tok_ref.at[:, lanes(f)], rows.at[own_z, lanes(f)], at_z(d)
            )

    send_tables()
    send_rows(0)

    flat = cache_ref[...].reshape(TOK, LAT)
    cq[...] = jnp.zeros_like(cq)
    for t in range(4):
        first = (group * 2 + c) * 4 + t
        hot = one_hot(iota((SLOTS, TOK), 1) == iota((SLOTS, TOK), 0) * BLK + first)
        cq[t, :, 0:LAT] = dot(hot, flat).astype(jnp.bfloat16)

    def piece(d, i):
        to = lax.rem(z + d, NZ)
        lane = pl.multiple_of(lax.rem(to, 2) * 256 + i * 128, 128)
        return cq.at[lax.div(to, 2), :, pl.ds(lane, 128)]

    def own_cz(i):
        return cz.at[i, pl.ds(pl.multiple_of(z * SLOTS, 16), SLOTS)]

    own_pieces = [
        pltpu.make_async_copy(piece(0, i), own_cz(i), local_sem.at[2 + i]) for i in range(PIECES)
    ]
    def send_pieces(i):
        own_pieces[i].start()
        for d in ALONG_Z:
            copies.start(("cz", i, d), piece(d, i), own_cz(i), at_z(d))

    send_rows(1)
    send_pieces(0)
    send_pieces(1)
    send_pieces(2)
    send_rows(2)

    at_row, at_lane = iota((2 * CHUNK, 2 * CHUNK), 0), iota((2 * CHUNK, 2 * CHUNK), 1)
    wanted = jnp.where(at_row < CHUNK, 2 * at_row, 2 * at_row - (2 * CHUNK - 1))
    perm[...] = one_hot(at_lane == wanted)

    def lay_out(first, last):
        @pl.loop(first, last)
        def step(k):
            at = pl.ds(pl.multiple_of(k * CHUNK, CHUNK), CHUNK)
            mixed = raw[at].reshape(2 * CHUNK, HID)
            apart = dot(perm[...], mixed).astype(jnp.bfloat16)
            wgu[at, 0:HID] = apart[:CHUNK]
            wgu[at, HID : 2 * HID] = apart[CHUNK:]

    src = source_ref[...].astype(jnp.float32)
    owner = over(src, SLOTS)
    src_x = over(owner, 16)
    in_x = owner - 16.0 * src_x
    src_z = over(in_x, 2)
    src_y = in_x - 2.0 * src_z
    other_y = jnp.abs(src_y - yh.astype(jnp.float32))
    at = (other_y * NZ + src_z) * SLOTS + (src - owner * SLOTS)
    pos[...] = jnp.where(src_x == x.astype(jnp.float32), at, -1.0)

    for d in ALONG_Z:
        copies.arrived(("meta", d))
    everyone = metag[0]
    for d in ALONG_Z:
        everyone = everyone + metag[d]
    ids, gates = everyone[0:8], everyone[8:16]
    hits, weights = [], []
    for e in OFFSETS:
        for rel in range(2):
            expert = (lax.rem(x + e, NX) * NZ + z) * 2 + (yh if rel == 0 else 1 - yh)
            equal = ids == expert.astype(jnp.float32)
            hits.append(jnp.max(jnp.where(equal, 1.0, 0.0), axis=0, keepdims=True))
            weights.append(jnp.sum(jnp.where(equal, gates, 0.0), axis=0, keepdims=True))
    hit = jnp.concatenate(hits, axis=0)
    before, after = iota((128, 128), 0), iota((128, 128), 1)
    earlier = one_hot(
        (lax.shift_right_logical(before, 4) == lax.shift_right_logical(after, 4))
        & (before < after)
    )
    rank = jnp.where(hit > 0.0, dot(hit.astype(jnp.bfloat16), earlier), -1.0)
    slot_at, row_at = iota((32, 128), 0), iota((32, 128), 1)
    same_source = lax.shift_right_logical(slot_at, 2) == lax.shift_right_logical(row_at, 4)
    slot_rank = lax.bitwise_and(slot_at, 3).astype(jnp.float32)
    for i in range(8):
        hot = same_source & (slot_rank == rank[i : i + 1])
        pick[i * 32 : i * 32 + 32] = one_hot(hot)
        selw[i * 32 : i * 32 + 32] = jnp.where(hot, weights[i], 0.0)

    def from_z(f):
        for d in ALONG_Z:
            copies.arrived(("tok", f, d))
        at = lanes(f)
        picked = dot(pick[...], rows[:, at]).astype(jnp.bfloat16)
        slots[tp, 0:32, at] = picked[0:32]
        other[0:32, at] = picked[32:64]
        along_y(f, 0, 32)
        xsend[:, at] = picked
        for p in (1, 2, 3):
            to, into = at_x(OFFSETS[p]), pl.ds(p * 32, 32)
            low, high = pl.ds(p * 64, 32), pl.ds(p * 64 + 32, 32)
            copies.start(("x0", f, p), xsend.at[low, at], slots.at[tp, into, at], to)
            copies.start(("x1", f, p), xsend.at[high, at], other.at[into, at], to)

    def along_y(f, first, count):
        at, low, high = lanes(f), pl.ds(first, count), pl.ds(128 + first, count)
        copies.start(
            ("near", f, first), slots.at[tp, low, at], slots.at[tp, low, at], near
        )
        copies.start(("cross", f, first), other.at[low, at], slots.at[tp, high, at], cross)
        copies.start(("far", f, first), other.at[low, at], slots.at[tp, high, at], far)

    def from_x(f):
        for p in (1, 2, 3):
            copies.arrived(("x0", f, p))
            copies.arrived(("x1", f, p))
        along_y(f, 32, 96)

    def from_y(f):
        at = lanes(f)
        for first in (0, 32):
            copies.arrived(("near", f, first))
            copies.arrived(("cross", f, first))
        copies.start(("core_n", f), slots.at[near_tp, :, at], slots.at[near_tp, :, at], core)
        for first in (0, 32):
            copies.arrived(("far", f, first))
        copies.start(("core_o", f), slots.at[tp, :, at], slots.at[tp, :, at], core)

    def gate_up(f):
        copies.arrived(("core_n", f))
        copies.arrived(("core_o", f))

        for k in range(4):
            more = dot(
                slots[k, :, lanes(f)], wgu[k * QF + STARTS[f] : k * QF + STARTS[f] + WIDTHS[f], :]
            )
            both[...] = more if f == 0 and k == 0 else both[...] + more

    def activate():
        gate, up = both[:, :HID], both[:, HID:]
        hidden[...] = (gate / (1.0 + jnp.exp(-gate)) * up).astype(jnp.bfloat16)

    def down(f):
        at = lanes(f)

        @pl.loop(0, 4)
        def step(k):
            row = pl.multiple_of(k * QF + STARTS[f], 128)
            part[lax.rem(k, 2), lax.div(k, 2), :, at] = lax.dot_general(
                hidden[...],
                wd[pl.ds(row, WIDTHS[f]), :],
                (((1,), (1,)), ((), ())),
                preferred_element_type=jnp.float32,
            ).astype(jnp.bfloat16)

        copies.start(("mate", f), part.at[1 - c, :, :, at], mate.at[:, :, at], core)

    def chip_sum(f):
        at = lanes(f)
        copies.arrived(("mate", f))
        for h in range(2):
            chip[h, :, at] = (
                part[c, h, :, at].astype(jnp.float32) + mate[h, :, at].astype(jnp.float32)
            ).astype(jnp.bfloat16)
        low, high = pl.ds(0, 128), pl.ds(128, 128)
        copies.start(("r_near", f), chip.at[1 - yl, low, at], back.at[0, :, at], near)
        copies.start(("r_cross", f), chip.at[1 - yl, high, at], back.at[1, :, at], cross)
        copies.start(("r_far", f), chip.at[yl, high, at], back.at[2, :, at], far)

    def expert_out(f):
        at = lanes(f)
        copies.arrived(("r_near", f))
        own = (
            chip[yl, 0:128, at].astype(jnp.float32) + back[0, :, at].astype(jnp.float32)
        ).astype(jnp.bfloat16)
        copies.arrived(("r_cross", f))
        copies.arrived(("r_far", f))
        rest = (
            back[1, :, at].astype(jnp.float32) + back[2, :, at].astype(jnp.float32)
        ).astype(jnp.bfloat16)
        for p in (1, 2, 3, 0):
            into = bbuf if p == 0 else ebuf
            into[p * 64 : p * 64 + 32, at] = own[p * 32 : p * 32 + 32]
            into[p * 64 + 32 : p * 64 + 64, at] = rest[p * 32 : p * 32 + 32]
            if p != 0:
                there = pl.ds(p * 64, 64)
                copies.start(
                    ("r_x", f, p), ebuf.at[there, at], bbuf.at[there, at], at_x(NX - OFFSETS[p])
                )

    def combine(f):
        at = lanes(f)
        for p in (1, 2, 3):
            copies.arrived(("r_x", f, p))
        wide = selw[...]
        high = wide.astype(jnp.bfloat16)
        low = (wide - high.astype(jnp.float32)).astype(jnp.bfloat16)
        contract = (((0,), (0,)), ((), ()))
        joined = bbuf[:, at]
        summed = lax.dot_general(high, joined, contract, preferred_element_type=jnp.float32)
        summed += lax.dot_general(low, joined, contract, preferred_element_type=jnp.float32)
        zsend[:, at] = summed.astype(jnp.bfloat16)
        for d in ALONG_Z:
            there = pl.ds(pl.multiple_of(lax.rem(z + NZ - d, NZ) * ROWS, ROWS), ROWS)
            copies.start(("z", f, d), zsend.at[there, at], zrecv.at[d, :, at], at_z(NZ - d))

    def total(f):
        at = lanes(f)
        out = zsend[own_z, at].astype(jnp.float32)
        for d in ALONG_Z:
            copies.arrived(("z", f, d))
            out += zrecv[d, :, at].astype(jnp.float32)
        moe_ref[:, at] = out.astype(jnp.bfloat16)

    def cache_swap(i):
        own_pieces[i].wait()
        for d in ALONG_Z:
            copies.arrived(("cz", i, d))
        first, second = pl.ds(0, HALF), pl.ds(HALF, HALF)
        copies.start(("swap", i), cz.at[i, first], cz.at[i, second], cross)

    def cache_hot(e):
        lane = iota((HALF, 128), 1).astype(jnp.float32)
        to = lax.rem(x + e, NX)
        for m in range(6):
            line = pos[pl.ds(to * 6 + m, 1), :]
            jb[m * 128 : m * 128 + 128] = jnp.broadcast_to(line, (128, 128)).T
        wants = jnp.concatenate(
            [jb[pl.ds(pl.multiple_of(i * 96 + yh * SLOTS, 16), SLOTS), :] for i in range(NZ)],
            axis=0,
        )
        for k in range(6):
            hots[e, :, k * 128 : k * 128 + 128] = one_hot(wants == lane + 128.0 * k)

    def cache_pick(i):
        copies.arrived(("swap", i))
        for e in (2, 1, 3, 0):
            found = dot(hots[e], cz[i]).astype(jnp.bfloat16)
            if e == 0:
                cxr[0, i] = found
            else:
                cxs[e, i] = found
                copies.start(("cx", i, e), cxs.at[e, i], cxr.at[e, i], at_x(e))

    def own_slots(i, d):
        start = pl.multiple_of(lax.rem(z + d, NZ) * SLOTS, 16)
        return cm.at[i, pl.ds(start, SLOTS)]

    def landing(i):
        lane = pl.multiple_of(lax.rem(z, 2) * 128 + i * 256, 128)
        return keys.at[group, c, lax.div(z, 2), :, pl.ds(lane, 128)]

    own_keys = {}

    def cache_merge(i):
        for e in (1, 3, 2):
            copies.arrived(("cx", i, e))
        cm[i] = (cxr[0, i] + cxr[1, i]) + (cxr[2, i] + cxr[3, i])
        own_keys[i] = pltpu.make_async_copy(
            own_slots(i, 0), landing(i), local_sem.at[2 + PIECES + i]
        )
        own_keys[i].start()
        for d in ALONG_Z:
            copies.start(("k", i, d), own_slots(i, d), landing(i), at_z(d))

    def key_lanes(i):
        return pl.ds(i * 256, 256) if i + 1 < PIECES else pl.ds(KL - 128, 128)

    def cache_tp(i):
        own_keys[i].wait()
        for d in ALONG_Z:
            copies.arrived(("k", i, d))
        there = keys.at[group, c, :, :, key_lanes(i)]
        copies.start(("k_near", i), there, there, near)
        copies.start(("k_core", i, 0), there, there, core)

    def cache_core(i):
        copies.arrived(("k_near", i))
        there = keys.at[1 - group, c, :, :, key_lanes(i)]
        copies.start(("k_core", i, 1), there, there, core)

    def place_queries():
        qp[...] = jnp.zeros_like(qp)
        flat_q = q_ref[...].reshape(256, LAT)
        for i in range(2):
            for h in range(2):
                entry, lane = h * 256 + i * 128, i * 256 + h * 128
                qp[:, lane : lane + 128] = flat_q[:, entry : entry + 128]
        qp[:, 640 : 640 + LAT - KV] = flat_q[:, KV:LAT]

    def attention():
        for i in range(PIECES):
            copies.arrived(("k_core", i, 0))
            copies.arrived(("k_core", i, 1))
        held = keys[...].reshape(TOK, KL)
        rows_with_rows = (((1,), (1,)), ((), ()))
        scores = lax.dot_general(
            qp[:, 0:KV], held[:, 0:KV], rows_with_rows, preferred_element_type=jnp.float32
        )
        scores += lax.dot_general(
            qp[:, KL - 128 : KL],
            held[:, KL - 128 : KL],
            rows_with_rows,
            preferred_element_type=jnp.float32,
        )
        scores *= score_scale
        at = iota((SLOTS, TOK), 1).astype(jnp.float32)
        token = over(at, SLOTS)
        spread = one_hot(at - token * SLOTS == iota((SLOTS, TOK), 0).astype(jnp.float32))
        numbers = jnp.concatenate(
            [
                jnp.broadcast_to(request_ref[...].astype(jnp.float32), (8, SLOTS)),
                jnp.broadcast_to(used_ref[...].astype(jnp.float32), (8, SLOTS)),
            ],
            axis=0,
        ).astype(jnp.bfloat16)
        told = dot(numbers, spread)
        request, used = told[0:1], told[8:9]
        request = jnp.where(token[0:1] < used, request, -1.0)
        row = lax.shift_right_logical(iota((256, TOK), 0), 4).astype(jnp.float32)
        scores = jnp.where(row == request, scores, -1e30)
        terms = jnp.exp(scores - jnp.max(scores, axis=1, keepdims=True))
        weights = (terms / jnp.sum(terms, axis=1, keepdims=True)).astype(jnp.bfloat16)
        attended = dot(weights, held[:, 0:KV]).astype(jnp.bfloat16)
        for i in range(2):
            for h in range(2):
                entry, lane = h * 256 + i * 128, i * 256 + h * 128
                att_ref[:, entry : entry + 128] = attended[:, lane : lane + 128]

    from_z(0)
    cache_hot(2)
    cache_hot(1)
    raw_copy.wait()
    from_x(0)
    from_z(1)
    cache_hot(3)
    cache_swap(0)
    cache_hot(0)
    from_x(1)
    cache_swap(1)
    from_z(2)
    cache_swap(2)
    lay_out(0, 8)
    from_x(2)
    lay_out(8, 14)
    from_y(0)
    cache_pick(0)
    cache_pick(1)
    cache_pick(2)
    lay_out(14, 22)
    from_y(1)
    lay_out(22, 28)
    gate_up(0)
    gate_up(1)
    from_y(2)
    wd_copy.wait()
    place_queries()
    gate_up(2)
    activate()
    down(2)
    down(1)
    chip_sum(2)
    down(0)
    chip_sum(1)
    chip_sum(0)
    cache_merge(0)
    cache_merge(1)
    cache_merge(2)
    expert_out(2)
    cache_tp(0)
    expert_out(1)
    cache_tp(1)
    combine(2)
    cache_tp(2)
    expert_out(0)
    cache_core(0)
    cache_core(1)
    combine(1)
    cache_core(2)
    attention()
    combine(0)
    total(2)
    total(1)
    total(0)
    copies.finish()


def hand_out(moe_ref, att_ref, moe_out, att_out):
    moe_out[...] = moe_ref[...]
    att_out[...] = att_ref[...]


def body(
    tokens,
    expert_ids,
    gate_weights,
    expert_gate_up,
    expert_down,
    queries,
    latent_cache,
    block_source,
    block_request,
    block_used,
):
    bf16, f32 = jnp.bfloat16, jnp.float32
    vmem = pl.BlockSpec(memory_space=pltpu.VMEM)
    anyspace = pl.BlockSpec(memory_space=pl.ANY)
    count = 7 + 3 * 37 + 63
    results = (
        jax.ShapeDtypeStruct((ROWS, QF), bf16),
        jax.ShapeDtypeStruct((256, KV), bf16),
    )
    moe, attended = pl.pallas_call(
        kernel,
        out_shape=results,
        in_specs=[vmem] * 8 + [anyspace] * 2,
        out_specs=(vmem, vmem),
        scratch_shapes=[
            pltpu.SemaphoreType.DMA((count,)),
            pltpu.SemaphoreType.DMA((count,)),
            pltpu.SemaphoreType.DMA((8,)),
            pltpu.VMEM((D, 2, HID), bf16),
            pltpu.VMEM((D, 2 * HID), bf16),
            pltpu.VMEM((D, HID), bf16),
            pltpu.VMEM((2 * CHUNK, 2 * CHUNK), bf16),
            pltpu.VMEM((16, 128), f32),
            pltpu.VMEM((NZ, 16, 128), f32),
            pltpu.VMEM((NZ * ROWS, QF), bf16),
            pltpu.VMEM((256, 128), bf16),
            pltpu.VMEM((256, 128), f32),
            pltpu.VMEM((256, QF), bf16),
            pltpu.VMEM((4, 256, QF), bf16),
            pltpu.VMEM((128, QF), bf16),
            pltpu.VMEM((256, 2 * HID), f32),
            pltpu.VMEM((256, HID), bf16),
            pltpu.VMEM((2, 2, 256, QF), bf16),
            pltpu.VMEM((2, 256, QF), bf16),
            pltpu.VMEM((2, 256, QF), bf16),
            pltpu.VMEM((3, 128, QF), bf16),
            pltpu.VMEM((256, QF), bf16),
            pltpu.VMEM((256, QF), bf16),
            pltpu.VMEM((NZ * ROWS, QF), bf16),
            pltpu.VMEM((NZ, ROWS, QF), bf16),
            pltpu.VMEM((4, SLOTS, 640), bf16),
            pltpu.VMEM((24, 128), f32),
            pltpu.VMEM((TOK, 128), f32),
            pltpu.VMEM((PIECES, 2 * HALF, 128), bf16),
            pltpu.VMEM((NX, HALF, 2 * HALF), bf16),
            pltpu.VMEM((NX, PIECES, HALF, 128), bf16),
            pltpu.VMEM((NX, PIECES, HALF, 128), bf16),
            pltpu.VMEM((PIECES, HALF, 128), bf16),
            pltpu.VMEM((2, 2, 4, SLOTS, KL), bf16),
            pltpu.VMEM((256, KL), bf16),
        ],
        compiler_params=pltpu.CompilerParams(
            collective_id=0, has_side_effects=True, vmem_limit_bytes=56 * 2**20
        ),
        cost_estimate=pl.CostEstimate(
            flops=8 * 10**9, bytes_accessed=13 * 10**6, transcendentals=3 * 10**5
        ),
        name="layer",
    )(
        expert_ids.T,
        gate_weights.T,
        tokens,
        latent_cache,
        block_source.reshape(24, 128),
        queries,
        block_request.reshape(1, SLOTS),
        block_used.reshape(1, SLOTS),
        expert_gate_up[0],
        expert_down[0],
    )
    moe, attended = pl.pallas_call(
        hand_out, out_shape=results, in_specs=[vmem] * 2, out_specs=(vmem, vmem), name="results"
    )(moe, attended)
    return moe, attended.reshape(ROWS, 16, KV)


def solution(mesh):
    placed = (
        P("ep", "tp"),
        P("ep", None),
        P("ep", None),
        P("ep", None, None, "tp"),
        P("ep", None, "tp"),
        P("ep", "tp", None),
        P("ep", None, None),
        P(),
        P("ep"),
        P("ep"),
    )
    return jax.shard_map(
        body,
        mesh=mesh,
        in_specs=placed,
        out_specs=(P("ep", "tp"), P("ep", "tp", None)),
        check_vma=False,
    )
```

```python
import jax
import jax.numpy as jnp
from jax import lax
from jax.experimental import pallas as pl
from jax.experimental.pallas import tpu as pltpu
from jax.sharding import PartitionSpec as P

MESH = pl.DeviceIdType.MESH

D = 7168
QF = 1792
HID = 256
ROWS = 16
NX, NZ = 4, 8
SLOTS = 48
HALF = NZ * SLOTS
BLK = 16
LAT = 576
KV = 512
PIECES = 3
KL = 2 * PIECES * 128
TOK = SLOTS * BLK
OFFSETS = (0, 1, 3, 2)
ALONG_Z = (4, 3, 5, 2, 6, 1, 7)
WIDTHS = (384, 640, 768)
STARTS = (0, 384, 1024)
OUT_RELAYED = (0, 1,)
CHUNK = 256

score_scale = 192.0 ** (-0.5)


def place():
    ep, tp = lax.axis_index("ep"), lax.axis_index("tp")
    x = lax.div(ep, 16)
    z = lax.rem(lax.div(ep, 2), NZ)
    return x, z, lax.rem(ep, 2), lax.div(tp, 2), lax.rem(tp, 2)


def device(x, z, yh, yl, c):
    return ((x * NZ + z) * 2 + yh, yl * 2 + c)


def iota(shape, axis):
    return lax.broadcasted_iota(jnp.int32, shape, axis)


def one_hot(equal):
    return jnp.where(equal, 1.0, 0.0).astype(jnp.bfloat16)


def over(values, divisor):
    return jnp.floor((values + 0.5) * (1.0 / divisor))


def dot(a, b):
    return jnp.dot(a, b, preferred_element_type=jnp.float32)


class Copies:
    def __init__(self, send, recv):
        self.send, self.recv, self.made, self.count = send, recv, {}, 0

    def start(self, name, src, dst, to):
        i = self.count
        self.count += 1
        copy = pltpu.make_async_remote_copy(
            src_ref=src,
            dst_ref=dst,
            send_sem=self.send.at[i],
            recv_sem=self.recv.at[i],
            device_id=to,
            device_id_type=MESH,
        )
        copy.start()
        self.made[name] = copy

    def arrived(self, name):
        self.made[name].wait_recv()

    def finish(self):
        for copy in self.made.values():
            copy.wait_send()


def kernel(
    ids_ref,
    gate_ref,
    tok_ref,
    cache_ref,
    source_ref,
    q_ref,
    request_ref,
    used_ref,
    wgu_ref,
    wd_ref,
    moe_ref,
    att_ref,
    send_sem,
    recv_sem,
    local_sem,
    raw,
    wgu,
    wd,
    perm,
    meta,
    metag,
    rows,
    pick,
    selw,
    xsend,
    slots,
    other,
    both,
    hidden,
    part,
    mate,
    chip,
    back,
    ebuf,
    bbuf,
    zsend,
    zrecv,
    cq,
    pos,
    jb,
    cz,
    hots,
    cxs,
    cxr,
    cm,
    keys,
    qp,
):
    x, z, yh, yl, c = place()
    tp = yl * 2 + c
    near_tp = (1 - yl) * 2 + c
    group = lax.rem(yl + yh, 2)
    copies = Copies(send_sem, recv_sem)

    def at_x(e):
        return device(lax.rem(x + e, NX), z, yh, yl, c)

    def at_z(d):
        return device(x, lax.rem(z + d, NZ), yh, yl, c)

    core = device(x, z, yh, yl, 1 - c)
    near = device(x, z, yh, 1 - yl, c)
    cross = device(x, z, 1 - yh, 1 - yl, c)
    far = device(x, z, 1 - yh, yl, c)

    barrier = pltpu.get_barrier_semaphore()
    partners = [at_x(e) for e in range(1, NX)] + [at_z(d) for d in range(1, NZ)]
    partners += [core, near, cross, far]
    for partner in partners:
        pl.semaphore_signal(barrier, inc=1, device_id=partner, device_id_type=MESH)

    raw_copy = pltpu.make_async_copy(wgu_ref, raw, local_sem.at[0])
    wd_copy = pltpu.make_async_copy(wd_ref, wd, local_sem.at[1])
    raw_copy.start()
    wd_copy.start()

    meta[...] = jnp.zeros_like(meta)
    meta[0:8, 0:ROWS] = ids_ref[...].astype(jnp.float32)
    meta[8:16, 0:ROWS] = gate_ref[...]
    to_lanes = jnp.where(iota((128, 128), 1) == iota((128, 128), 0) + z * ROWS, 1.0, 0.0)
    meta[...] = jnp.dot(
        meta[...],
        to_lanes,
        precision=lax.Precision.HIGHEST,
        preferred_element_type=jnp.float32,
    )
    metag[0] = meta[...]
    own_z = pl.ds(pl.multiple_of(z * ROWS, ROWS), ROWS)
    rows[own_z, :] = tok_ref[...]
    pl.semaphore_wait(barrier, len(partners))

    def lanes(f):
        return pl.ds(STARTS[f], WIDTHS[f])

    def send_tables():
        for d in ALONG_Z:
            copies.start(("meta", d), meta, metag.at[d], at_z(d))

    def send_rows(f):
        for d in ALONG_Z:
            copies.start(
                ("tok", f, d), tok_ref.at[:, lanes(f)], rows.at[own_z, lanes(f)], at_z(d)
            )

    send_tables()
    send_rows(0)

    flat = cache_ref[...].reshape(TOK, LAT)
    cq[...] = jnp.zeros_like(cq)
    for t in range(4):
        first = (group * 2 + c) * 4 + t
        hot = one_hot(iota((SLOTS, TOK), 1) == iota((SLOTS, TOK), 0) * BLK + first)
        cq[t, :, 0:LAT] = dot(hot, flat).astype(jnp.bfloat16)

    def piece(d, i):
        to = lax.rem(z + d, NZ)
        lane = pl.multiple_of(lax.rem(to, 2) * 256 + i * 128, 128)
        return cq.at[lax.div(to, 2), :, pl.ds(lane, 128)]

    def own_cz(i):
        return cz.at[i, pl.ds(pl.multiple_of(z * SLOTS, 16), SLOTS)]

    own_pieces = [
        pltpu.make_async_copy(piece(0, i), own_cz(i), local_sem.at[2 + i]) for i in range(PIECES)
    ]
    def send_pieces(i):
        own_pieces[i].start()
        for d in ALONG_Z:
            copies.start(("cz", i, d), piece(d, i), own_cz(i), at_z(d))

    send_rows(1)
    send_pieces(0)
    send_pieces(1)
    send_pieces(2)
    send_rows(2)

    at_row, at_lane = iota((2 * CHUNK, 2 * CHUNK), 0), iota((2 * CHUNK, 2 * CHUNK), 1)
    wanted = jnp.where(at_row < CHUNK, 2 * at_row, 2 * at_row - (2 * CHUNK - 1))
    perm[...] = one_hot(at_lane == wanted)

    def lay_out(first, last):
        @pl.loop(first, last)
        def step(k):
            at = pl.ds(pl.multiple_of(k * CHUNK, CHUNK), CHUNK)
            mixed = raw[at].reshape(2 * CHUNK, HID)
            apart = dot(perm[...], mixed).astype(jnp.bfloat16)
            wgu[at, 0:HID] = apart[:CHUNK]
            wgu[at, HID : 2 * HID] = apart[CHUNK:]

    src = source_ref[...].astype(jnp.float32)
    owner = over(src, SLOTS)
    src_x = over(owner, 16)
    in_x = owner - 16.0 * src_x
    src_z = over(in_x, 2)
    src_y = in_x - 2.0 * src_z
    other_y = jnp.abs(src_y - yh.astype(jnp.float32))
    at = (other_y * NZ + src_z) * SLOTS + (src - owner * SLOTS)
    pos[...] = jnp.where(src_x == x.astype(jnp.float32), at, -1.0)

    for d in ALONG_Z:
        copies.arrived(("meta", d))
    everyone = metag[0]
    for d in ALONG_Z:
        everyone = everyone + metag[d]
    ids, gates = everyone[0:8], everyone[8:16]
    hits, weights = [], []
    for e in OFFSETS:
        for rel in range(2):
            expert = (lax.rem(x + e, NX) * NZ + z) * 2 + (yh if rel == 0 else 1 - yh)
            equal = ids == expert.astype(jnp.float32)
            hits.append(jnp.max(jnp.where(equal, 1.0, 0.0), axis=0, keepdims=True))
            weights.append(jnp.sum(jnp.where(equal, gates, 0.0), axis=0, keepdims=True))
    hit = jnp.concatenate(hits, axis=0)
    before, after = iota((128, 128), 0), iota((128, 128), 1)
    earlier = one_hot(
        (lax.shift_right_logical(before, 4) == lax.shift_right_logical(after, 4))
        & (before < after)
    )
    rank = jnp.where(hit > 0.0, dot(hit.astype(jnp.bfloat16), earlier), -1.0)
    slot_at, row_at = iota((32, 128), 0), iota((32, 128), 1)
    same_source = lax.shift_right_logical(slot_at, 2) == lax.shift_right_logical(row_at, 4)
    slot_rank = lax.bitwise_and(slot_at, 3).astype(jnp.float32)
    for i in range(8):
        hot = same_source & (slot_rank == rank[i : i + 1])
        pick[i * 32 : i * 32 + 32] = one_hot(hot)
        selw[i * 32 : i * 32 + 32] = jnp.where(hot, weights[i], 0.0)

    def from_z(f):
        for d in ALONG_Z:
            copies.arrived(("tok", f, d))
        at = lanes(f)
        picked = dot(pick[...], rows[:, at]).astype(jnp.bfloat16)
        slots[tp, 0:32, at] = picked[0:32]
        other[0:32, at] = picked[32:64]
        along_y(f, 0, 32)
        xsend[:, at] = picked
        for p in (1, 2, 3):
            to, into = at_x(OFFSETS[p]), pl.ds(p * 32, 32)
            low, high = pl.ds(p * 64, 32), pl.ds(p * 64 + 32, 32)
            copies.start(("x0", f, p), xsend.at[low, at], slots.at[tp, into, at], to)
            copies.start(("x1", f, p), xsend.at[high, at], other.at[into, at], to)

    def along_y(f, first, count):
        at, low, high = lanes(f), pl.ds(first, count), pl.ds(128 + first, count)
        copies.start(
            ("near", f, first), slots.at[tp, low, at], slots.at[tp, low, at], near
        )
        copies.start(("cross", f, first), other.at[low, at], slots.at[tp, high, at], cross)
        if f not in OUT_RELAYED:
            copies.start(("far", f, first), other.at[low, at], slots.at[tp, high, at], far)

    def from_x(f):
        for p in (1, 2, 3):
            copies.arrived(("x0", f, p))
            copies.arrived(("x1", f, p))
        along_y(f, 32, 96)

    def relay(f):
        at = lanes(f)
        for first in (0, 32):
            copies.arrived(("cross", f, first))
        there = slots.at[near_tp, pl.ds(128, 128), at]
        copies.start(("relay", f), there, there, near)

    def from_y(f):
        at = lanes(f)
        for first in (0, 32):
            copies.arrived(("near", f, first))
            if f not in OUT_RELAYED:
                copies.arrived(("cross", f, first))
        copies.start(("core_n", f), slots.at[near_tp, :, at], slots.at[near_tp, :, at], core)
        if f in OUT_RELAYED:
            copies.arrived(("relay", f))
        else:
            for first in (0, 32):
                copies.arrived(("far", f, first))
        copies.start(("core_o", f), slots.at[tp, :, at], slots.at[tp, :, at], core)

    def gate_up(f):
        copies.arrived(("core_n", f))
        copies.arrived(("core_o", f))

        for k in range(4):
            more = dot(
                slots[k, :, lanes(f)], wgu[k * QF + STARTS[f] : k * QF + STARTS[f] + WIDTHS[f], :]
            )
            both[...] = more if f == 0 and k == 0 else both[...] + more

    def activate():
        gate, up = both[:, :HID], both[:, HID:]
        hidden[...] = (gate / (1.0 + jnp.exp(-gate)) * up).astype(jnp.bfloat16)

    def down(f):
        at = lanes(f)

        @pl.loop(0, 4)
        def step(k):
            row = pl.multiple_of(k * QF + STARTS[f], 128)
            part[lax.rem(k, 2), lax.div(k, 2), :, at] = lax.dot_general(
                hidden[...],
                wd[pl.ds(row, WIDTHS[f]), :],
                (((1,), (1,)), ((), ())),
                preferred_element_type=jnp.float32,
            ).astype(jnp.bfloat16)

        copies.start(("mate", f), part.at[1 - c, :, :, at], mate.at[:, :, at], core)

    def chip_sum(f):
        at = lanes(f)
        copies.arrived(("mate", f))
        for h in range(2):
            chip[h, :, at] = (
                part[c, h, :, at].astype(jnp.float32) + mate[h, :, at].astype(jnp.float32)
            ).astype(jnp.bfloat16)
        low, high = pl.ds(0, 128), pl.ds(128, 128)
        copies.start(("r_cross", f), chip.at[1 - yl, high, at], back.at[1, :, at], cross)
        copies.start(("r_far", f), chip.at[yl, high, at], back.at[2, :, at], far)
        copies.start(("r_near", f), chip.at[1 - yl, low, at], back.at[0, :, at], near)

    def expert_out(f):
        at = lanes(f)
        copies.arrived(("r_near", f))
        own = (
            chip[yl, 0:128, at].astype(jnp.float32) + back[0, :, at].astype(jnp.float32)
        ).astype(jnp.bfloat16)
        copies.arrived(("r_cross", f))
        copies.arrived(("r_far", f))
        rest = (
            back[1, :, at].astype(jnp.float32) + back[2, :, at].astype(jnp.float32)
        ).astype(jnp.bfloat16)
        for p in (1, 2, 3, 0):
            into = bbuf if p == 0 else ebuf
            into[p * 64 : p * 64 + 32, at] = own[p * 32 : p * 32 + 32]
            into[p * 64 + 32 : p * 64 + 64, at] = rest[p * 32 : p * 32 + 32]
            if p != 0:
                there = pl.ds(p * 64, 64)
                copies.start(
                    ("r_x", f, p), ebuf.at[there, at], bbuf.at[there, at], at_x(NX - OFFSETS[p])
                )

    def combine(f):
        at = lanes(f)
        for p in (1, 2, 3):
            copies.arrived(("r_x", f, p))
        wide = selw[...]
        high = wide.astype(jnp.bfloat16)
        low = (wide - high.astype(jnp.float32)).astype(jnp.bfloat16)
        contract = (((0,), (0,)), ((), ()))
        joined = bbuf[:, at]
        summed = lax.dot_general(high, joined, contract, preferred_element_type=jnp.float32)
        summed += lax.dot_general(low, joined, contract, preferred_element_type=jnp.float32)
        zsend[:, at] = summed.astype(jnp.bfloat16)
        for d in ALONG_Z:
            there = pl.ds(pl.multiple_of(lax.rem(z + NZ - d, NZ) * ROWS, ROWS), ROWS)
            copies.start(("z", f, d), zsend.at[there, at], zrecv.at[d, :, at], at_z(NZ - d))

    def total(f):
        at = lanes(f)
        out = zsend[own_z, at].astype(jnp.float32)
        for d in ALONG_Z:
            copies.arrived(("z", f, d))
            out += zrecv[d, :, at].astype(jnp.float32)
        moe_ref[:, at] = out.astype(jnp.bfloat16)

    def cache_swap(i):
        own_pieces[i].wait()
        for d in ALONG_Z:
            copies.arrived(("cz", i, d))
        first, second = pl.ds(0, HALF), pl.ds(HALF, HALF)
        copies.start(("swap", i), cz.at[i, first], cz.at[i, second], cross)

    def cache_hot(e):
        lane = iota((HALF, 128), 1).astype(jnp.float32)
        to = lax.rem(x + e, NX)
        for m in range(6):
            line = pos[pl.ds(to * 6 + m, 1), :]
            jb[m * 128 : m * 128 + 128] = jnp.broadcast_to(line, (128, 128)).T
        wants = jnp.concatenate(
            [jb[pl.ds(pl.multiple_of(i * 96 + yh * SLOTS, 16), SLOTS), :] for i in range(NZ)],
            axis=0,
        )
        for k in range(6):
            hots[e, :, k * 128 : k * 128 + 128] = one_hot(wants == lane + 128.0 * k)

    def cache_pick(i):
        copies.arrived(("swap", i))
        for e in (2, 1, 3, 0):
            found = dot(hots[e], cz[i]).astype(jnp.bfloat16)
            if e == 0:
                cxr[0, i] = found
            else:
                cxs[e, i] = found
                copies.start(("cx", i, e), cxs.at[e, i], cxr.at[e, i], at_x(e))

    def own_slots(i, d):
        start = pl.multiple_of(lax.rem(z + d, NZ) * SLOTS, 16)
        return cm.at[i, pl.ds(start, SLOTS)]

    def landing(i):
        lane = pl.multiple_of(lax.rem(z, 2) * 128 + i * 256, 128)
        return keys.at[group, c, lax.div(z, 2), :, pl.ds(lane, 128)]

    own_keys = {}

    def cache_merge(i):
        for e in (1, 3, 2):
            copies.arrived(("cx", i, e))
        cm[i] = (cxr[0, i] + cxr[1, i]) + (cxr[2, i] + cxr[3, i])
        own_keys[i] = pltpu.make_async_copy(
            own_slots(i, 0), landing(i), local_sem.at[2 + PIECES + i]
        )
        own_keys[i].start()
        for d in ALONG_Z:
            copies.start(("k", i, d), own_slots(i, d), landing(i), at_z(d))

    def key_lanes(i):
        return pl.ds(i * 256, 256) if i + 1 < PIECES else pl.ds(KL - 128, 128)

    def cache_tp(i):
        own_keys[i].wait()
        for d in ALONG_Z:
            copies.arrived(("k", i, d))
        there = keys.at[group, c, :, :, key_lanes(i)]
        copies.start(("k_near", i), there, there, near)
        copies.start(("k_core", i, 0), there, there, core)

    def cache_core(i):
        copies.arrived(("k_near", i))
        there = keys.at[1 - group, c, :, :, key_lanes(i)]
        copies.start(("k_core", i, 1), there, there, core)

    def place_queries():
        qp[...] = jnp.zeros_like(qp)
        flat_q = q_ref[...].reshape(256, LAT)
        for i in range(2):
            for h in range(2):
                entry, lane = h * 256 + i * 128, i * 256 + h * 128
                qp[:, lane : lane + 128] = flat_q[:, entry : entry + 128]
        qp[:, 640 : 640 + LAT - KV] = flat_q[:, KV:LAT]

    def attention():
        for i in range(PIECES):
            copies.arrived(("k_core", i, 0))
            copies.arrived(("k_core", i, 1))
        held = keys[...].reshape(TOK, KL)
        rows_with_rows = (((1,), (1,)), ((), ()))
        scores = lax.dot_general(
            qp[:, 0:KV], held[:, 0:KV], rows_with_rows, preferred_element_type=jnp.float32
        )
        scores += lax.dot_general(
            qp[:, KL - 128 : KL],
            held[:, KL - 128 : KL],
            rows_with_rows,
            preferred_element_type=jnp.float32,
        )
        scores *= score_scale
        at = iota((SLOTS, TOK), 1).astype(jnp.float32)
        token = over(at, SLOTS)
        spread = one_hot(at - token * SLOTS == iota((SLOTS, TOK), 0).astype(jnp.float32))
        numbers = jnp.concatenate(
            [
                jnp.broadcast_to(request_ref[...].astype(jnp.float32), (8, SLOTS)),
                jnp.broadcast_to(used_ref[...].astype(jnp.float32), (8, SLOTS)),
            ],
            axis=0,
        ).astype(jnp.bfloat16)
        told = dot(numbers, spread)
        request, used = told[0:1], told[8:9]
        request = jnp.where(token[0:1] < used, request, -1.0)
        row = lax.shift_right_logical(iota((256, TOK), 0), 4).astype(jnp.float32)
        scores = jnp.where(row == request, scores, -1e30)
        terms = jnp.exp(scores - jnp.max(scores, axis=1, keepdims=True))
        weights = (terms / jnp.sum(terms, axis=1, keepdims=True)).astype(jnp.bfloat16)
        attended = dot(weights, held[:, 0:KV]).astype(jnp.bfloat16)
        for i in range(2):
            for h in range(2):
                entry, lane = h * 256 + i * 128, i * 256 + h * 128
                att_ref[:, entry : entry + 128] = attended[:, lane : lane + 128]

    from_z(0)
    cache_hot(2)
    cache_hot(1)
    raw_copy.wait()
    from_x(0)
    from_z(1)
    cache_hot(3)
    cache_swap(0)
    cache_hot(0)
    from_x(1)
    cache_swap(1)
    relay(0)
    from_z(2)
    cache_swap(2)
    lay_out(0, 8)
    from_x(2)
    relay(1)
    lay_out(8, 12)
    from_y(0)
    cache_pick(0)
    cache_pick(1)
    lay_out(12, 22)
    from_y(1)
    cache_pick(2)
    lay_out(22, 28)
    gate_up(0)
    gate_up(1)
    from_y(2)
    wd_copy.wait()
    place_queries()
    gate_up(2)
    activate()
    down(2)
    chip_sum(2)
    down(1)
    chip_sum(1)
    down(0)
    chip_sum(0)
    cache_merge(0)
    cache_merge(1)
    cache_merge(2)
    expert_out(2)
    expert_out(1)
    combine(2)
    cache_tp(0)
    expert_out(0)
    cache_tp(1)
    combine(1)
    cache_tp(2)
    cache_core(0)
    combine(0)
    cache_core(1)
    cache_core(2)
    attention()
    total(2)
    total(1)
    total(0)
    copies.finish()


def hand_out(moe_ref, att_ref, moe_out, att_out):
    moe_out[...] = moe_ref[...]
    att_out[...] = att_ref[...]


def body(
    tokens,
    expert_ids,
    gate_weights,
    expert_gate_up,
    expert_down,
    queries,
    latent_cache,
    block_source,
    block_request,
    block_used,
):
    bf16, f32 = jnp.bfloat16, jnp.float32
    vmem = pl.BlockSpec(memory_space=pltpu.VMEM)
    anyspace = pl.BlockSpec(memory_space=pl.ANY)
    count = 7 + 3 * 37 + 63
    results = (
        jax.ShapeDtypeStruct((ROWS, QF), bf16),
        jax.ShapeDtypeStruct((256, KV), bf16),
    )
    moe, attended = pl.pallas_call(
        kernel,
        out_shape=results,
        in_specs=[vmem] * 8 + [anyspace] * 2,
        out_specs=(vmem, vmem),
        scratch_shapes=[
            pltpu.SemaphoreType.DMA((count,)),
            pltpu.SemaphoreType.DMA((count,)),
            pltpu.SemaphoreType.DMA((8,)),
            pltpu.VMEM((D, 2, HID), bf16),
            pltpu.VMEM((D, 2 * HID), bf16),
            pltpu.VMEM((D, HID), bf16),
            pltpu.VMEM((2 * CHUNK, 2 * CHUNK), bf16),
            pltpu.VMEM((16, 128), f32),
            pltpu.VMEM((NZ, 16, 128), f32),
            pltpu.VMEM((NZ * ROWS, QF), bf16),
            pltpu.VMEM((256, 128), bf16),
            pltpu.VMEM((256, 128), f32),
            pltpu.VMEM((256, QF), bf16),
            pltpu.VMEM((4, 256, QF), bf16),
            pltpu.VMEM((128, QF), bf16),
            pltpu.VMEM((256, 2 * HID), f32),
            pltpu.VMEM((256, HID), bf16),
            pltpu.VMEM((2, 2, 256, QF), bf16),
            pltpu.VMEM((2, 256, QF), bf16),
            pltpu.VMEM((2, 256, QF), bf16),
            pltpu.VMEM((3, 128, QF), bf16),
            pltpu.VMEM((256, QF), bf16),
            pltpu.VMEM((256, QF), bf16),
            pltpu.VMEM((NZ * ROWS, QF), bf16),
            pltpu.VMEM((NZ, ROWS, QF), bf16),
            pltpu.VMEM((4, SLOTS, 640), bf16),
            pltpu.VMEM((24, 128), f32),
            pltpu.VMEM((TOK, 128), f32),
            pltpu.VMEM((PIECES, 2 * HALF, 128), bf16),
            pltpu.VMEM((NX, HALF, 2 * HALF), bf16),
            pltpu.VMEM((NX, PIECES, HALF, 128), bf16),
            pltpu.VMEM((NX, PIECES, HALF, 128), bf16),
            pltpu.VMEM((PIECES, HALF, 128), bf16),
            pltpu.VMEM((2, 2, 4, SLOTS, KL), bf16),
            pltpu.VMEM((256, KL), bf16),
        ],
        compiler_params=pltpu.CompilerParams(
            collective_id=0, has_side_effects=True, vmem_limit_bytes=56 * 2**20
        ),
        cost_estimate=pl.CostEstimate(
            flops=8 * 10**9, bytes_accessed=13 * 10**6, transcendentals=3 * 10**5
        ),
        name="layer",
    )(
        expert_ids.T,
        gate_weights.T,
        tokens,
        latent_cache,
        block_source.reshape(24, 128),
        queries,
        block_request.reshape(1, SLOTS),
        block_used.reshape(1, SLOTS),
        expert_gate_up[0],
        expert_down[0],
    )
    moe, attended = pl.pallas_call(
        hand_out, out_shape=results, in_specs=[vmem] * 2, out_specs=(vmem, vmem), name="results"
    )(moe, attended)
    return moe, attended.reshape(ROWS, 16, KV)


def solution(mesh):
    placed = (
        P("ep", "tp"),
        P("ep", None),
        P("ep", None),
        P("ep", None, None, "tp"),
        P("ep", None, "tp"),
        P("ep", "tp", None),
        P("ep", None, None),
        P(),
        P("ep"),
        P("ep"),
    )
    return jax.shard_map(
        body,
        mesh=mesh,
        in_specs=placed,
        out_specs=(P("ep", "tp"), P("ep", "tp", None)),
        check_vma=False,
    )
```

```python
import jax
import jax.numpy as jnp
from jax import lax
from jax.experimental import pallas as pl
from jax.experimental.pallas import tpu as pltpu
from jax.sharding import PartitionSpec as P

MESH = pl.DeviceIdType.MESH

D = 7168
QF = 1792
HID = 256
ROWS = 16
NX, NZ = 4, 8
SLOTS = 48
HALF = NZ * SLOTS
BLK = 16
LAT = 576
KV = 512
PIECES = 3
KL = 2 * PIECES * 128
TOK = SLOTS * BLK
OFFSETS = (0, 1, 3, 2)
ALONG_Z = (4, 3, 5, 2, 6, 1, 7)
WIDTHS = (384, 768, 640)
STARTS = (0, 384, 1152)
OUT_RELAYED = (0, 1,)
CHUNK = 256

score_scale = 192.0 ** (-0.5)


def place():
    ep, tp = lax.axis_index("ep"), lax.axis_index("tp")
    x = lax.div(ep, 16)
    z = lax.rem(lax.div(ep, 2), NZ)
    return x, z, lax.rem(ep, 2), lax.div(tp, 2), lax.rem(tp, 2)


def device(x, z, yh, yl, c):
    return ((x * NZ + z) * 2 + yh, yl * 2 + c)


def iota(shape, axis):
    return lax.broadcasted_iota(jnp.int32, shape, axis)


def one_hot(equal):
    return jnp.where(equal, 1.0, 0.0).astype(jnp.bfloat16)


def over(values, divisor):
    return jnp.floor((values + 0.5) * (1.0 / divisor))


def dot(a, b):
    return jnp.dot(a, b, preferred_element_type=jnp.float32)


class Copies:
    def __init__(self, send, recv):
        self.send, self.recv, self.made, self.count = send, recv, {}, 0

    def start(self, name, src, dst, to):
        i = self.count
        self.count += 1
        copy = pltpu.make_async_remote_copy(
            src_ref=src,
            dst_ref=dst,
            send_sem=self.send.at[i],
            recv_sem=self.recv.at[i],
            device_id=to,
            device_id_type=MESH,
        )
        copy.start()
        self.made[name] = copy

    def arrived(self, name):
        self.made[name].wait_recv()

    def finish(self):
        for copy in self.made.values():
            copy.wait_send()


def kernel(
    ids_ref,
    gate_ref,
    tok_ref,
    cache_ref,
    source_ref,
    q_ref,
    request_ref,
    used_ref,
    wgu_ref,
    wd_ref,
    moe_ref,
    att_ref,
    send_sem,
    recv_sem,
    local_sem,
    raw,
    wgu,
    wd,
    perm,
    meta,
    metag,
    rows,
    pick,
    selw,
    xsend,
    slots,
    other,
    both,
    hidden,
    part,
    mate,
    chip,
    back,
    ebuf,
    bbuf,
    zsend,
    zrecv,
    cq,
    pos,
    jb,
    cz,
    hots,
    cxs,
    cxr,
    cm,
    keys,
    qp,
):
    x, z, yh, yl, c = place()
    tp = yl * 2 + c
    near_tp = (1 - yl) * 2 + c
    group = lax.rem(yl + yh, 2)
    copies = Copies(send_sem, recv_sem)

    def at_x(e):
        return device(lax.rem(x + e, NX), z, yh, yl, c)

    def at_z(d):
        return device(x, lax.rem(z + d, NZ), yh, yl, c)

    core = device(x, z, yh, yl, 1 - c)
    near = device(x, z, yh, 1 - yl, c)
    cross = device(x, z, 1 - yh, 1 - yl, c)
    far = device(x, z, 1 - yh, yl, c)

    barrier = pltpu.get_barrier_semaphore()
    partners = [at_x(e) for e in range(1, NX)] + [at_z(d) for d in range(1, NZ)]
    partners += [core, near, cross, far]
    for partner in partners:
        pl.semaphore_signal(barrier, inc=1, device_id=partner, device_id_type=MESH)

    raw_copy = pltpu.make_async_copy(wgu_ref, raw, local_sem.at[0])
    wd_copy = pltpu.make_async_copy(wd_ref, wd, local_sem.at[1])
    raw_copy.start()
    wd_copy.start()

    meta[...] = jnp.zeros_like(meta)
    meta[0:8, 0:ROWS] = ids_ref[...].astype(jnp.float32)
    meta[8:16, 0:ROWS] = gate_ref[...]
    to_lanes = jnp.where(iota((128, 128), 1) == iota((128, 128), 0) + z * ROWS, 1.0, 0.0)
    meta[...] = jnp.dot(
        meta[...],
        to_lanes,
        precision=lax.Precision.HIGHEST,
        preferred_element_type=jnp.float32,
    )
    metag[0] = meta[...]
    own_z = pl.ds(pl.multiple_of(z * ROWS, ROWS), ROWS)
    rows[own_z, :] = tok_ref[...]
    pl.semaphore_wait(barrier, len(partners))

    def lanes(f):
        return pl.ds(STARTS[f], WIDTHS[f])

    def send_tables():
        for d in ALONG_Z:
            copies.start(("meta", d), meta, metag.at[d], at_z(d))

    def send_rows(f):
        for d in ALONG_Z:
            copies.start(
                ("tok", f, d), tok_ref.at[:, lanes(f)], rows.at[own_z, lanes(f)], at_z(d)
            )

    send_rows(0)
    send_tables()

    flat = cache_ref[...].reshape(TOK, LAT)
    cq[...] = jnp.zeros_like(cq)
    for t in range(4):
        first = (group * 2 + c) * 4 + t
        hot = one_hot(iota((SLOTS, TOK), 1) == iota((SLOTS, TOK), 0) * BLK + first)
        cq[t, :, 0:LAT] = dot(hot, flat).astype(jnp.bfloat16)

    def piece(d, i):
        to = lax.rem(z + d, NZ)
        lane = pl.multiple_of(lax.rem(to, 2) * 256 + i * 128, 128)
        return cq.at[lax.div(to, 2), :, pl.ds(lane, 128)]

    def own_cz(i):
        return cz.at[i, pl.ds(pl.multiple_of(z * SLOTS, 16), SLOTS)]

    own_pieces = [
        pltpu.make_async_copy(piece(0, i), own_cz(i), local_sem.at[2 + i]) for i in range(PIECES)
    ]
    def send_pieces(i):
        own_pieces[i].start()
        for d in ALONG_Z:
            copies.start(("cz", i, d), piece(d, i), own_cz(i), at_z(d))

    send_rows(1)
    send_pieces(0)
    send_pieces(1)
    send_pieces(2)
    send_rows(2)

    at_row, at_lane = iota((2 * CHUNK, 2 * CHUNK), 0), iota((2 * CHUNK, 2 * CHUNK), 1)
    wanted = jnp.where(at_row < CHUNK, 2 * at_row, 2 * at_row - (2 * CHUNK - 1))
    perm[...] = one_hot(at_lane == wanted)

    def lay_out(first, last):
        @pl.loop(first, last)
        def step(k):
            at = pl.ds(pl.multiple_of(k * CHUNK, CHUNK), CHUNK)
            mixed = raw[at].reshape(2 * CHUNK, HID)
            apart = dot(perm[...], mixed).astype(jnp.bfloat16)
            wgu[at, 0:HID] = apart[:CHUNK]
            wgu[at, HID : 2 * HID] = apart[CHUNK:]

    src = source_ref[...].astype(jnp.float32)
    owner = over(src, SLOTS)
    src_x = over(owner, 16)
    in_x = owner - 16.0 * src_x
    src_z = over(in_x, 2)
    src_y = in_x - 2.0 * src_z
    other_y = jnp.abs(src_y - yh.astype(jnp.float32))
    at = (other_y * NZ + src_z) * SLOTS + (src - owner * SLOTS)
    pos[...] = jnp.where(src_x == x.astype(jnp.float32), at, -1.0)

    for d in ALONG_Z:
        copies.arrived(("meta", d))
    everyone = metag[0]
    for d in ALONG_Z:
        everyone = everyone + metag[d]
    ids, gates = everyone[0:8], everyone[8:16]
    hits, weights = [], []
    for e in OFFSETS:
        for rel in range(2):
            expert = (lax.rem(x + e, NX) * NZ + z) * 2 + (yh if rel == 0 else 1 - yh)
            equal = ids == expert.astype(jnp.float32)
            hits.append(jnp.max(jnp.where(equal, 1.0, 0.0), axis=0, keepdims=True))
            weights.append(jnp.sum(jnp.where(equal, gates, 0.0), axis=0, keepdims=True))
    hit = jnp.concatenate(hits, axis=0)
    before, after = iota((128, 128), 0), iota((128, 128), 1)
    earlier = one_hot(
        (lax.shift_right_logical(before, 4) == lax.shift_right_logical(after, 4))
        & (before < after)
    )
    rank = jnp.where(hit > 0.0, dot(hit.astype(jnp.bfloat16), earlier), -1.0)
    slot_at, row_at = iota((32, 128), 0), iota((32, 128), 1)
    same_source = lax.shift_right_logical(slot_at, 2) == lax.shift_right_logical(row_at, 4)
    slot_rank = lax.bitwise_and(slot_at, 3).astype(jnp.float32)
    for i in range(8):
        hot = same_source & (slot_rank == rank[i : i + 1])
        pick[i * 32 : i * 32 + 32] = one_hot(hot)
        selw[i * 32 : i * 32 + 32] = jnp.where(hot, weights[i], 0.0)

    def from_z(f):
        for d in ALONG_Z:
            copies.arrived(("tok", f, d))
        at = lanes(f)
        picked = dot(pick[...], rows[:, at]).astype(jnp.bfloat16)
        slots[tp, 0:32, at] = picked[0:32]
        other[0:32, at] = picked[32:64]
        along_y(f, 0, 32)
        xsend[:, at] = picked
        for p in (1, 2, 3):
            to, into = at_x(OFFSETS[p]), pl.ds(p * 32, 32)
            low, high = pl.ds(p * 64, 32), pl.ds(p * 64 + 32, 32)
            copies.start(("x0", f, p), xsend.at[low, at], slots.at[tp, into, at], to)
            copies.start(("x1", f, p), xsend.at[high, at], other.at[into, at], to)

    def along_y(f, first, count):
        at, low, high = lanes(f), pl.ds(first, count), pl.ds(128 + first, count)
        copies.start(
            ("near", f, first), slots.at[tp, low, at], slots.at[tp, low, at], near
        )
        copies.start(("cross", f, first), other.at[low, at], slots.at[tp, high, at], cross)
        if f not in OUT_RELAYED:
            copies.start(("far", f, first), other.at[low, at], slots.at[tp, high, at], far)

    def from_x(f):
        for p in (1, 2, 3):
            copies.arrived(("x0", f, p))
            copies.arrived(("x1", f, p))
        along_y(f, 32, 96)

    def relay(f):
        at = lanes(f)
        for first in (0, 32):
            copies.arrived(("cross", f, first))
        there = slots.at[near_tp, pl.ds(128, 128), at]
        copies.start(("relay", f), there, there, near)

    def from_y(f):
        at = lanes(f)
        for first in (0, 32):
            copies.arrived(("near", f, first))
            if f not in OUT_RELAYED:
                copies.arrived(("cross", f, first))
        copies.start(("core_n", f), slots.at[near_tp, :, at], slots.at[near_tp, :, at], core)
        if f in OUT_RELAYED:
            copies.arrived(("relay", f))
        else:
            for first in (0, 32):
                copies.arrived(("far", f, first))
        copies.start(("core_o", f), slots.at[tp, :, at], slots.at[tp, :, at], core)

    def gate_up(f):
        copies.arrived(("core_n", f))
        copies.arrived(("core_o", f))

        for k in range(4):
            more = dot(
                slots[k, :, lanes(f)], wgu[k * QF + STARTS[f] : k * QF + STARTS[f] + WIDTHS[f], :]
            )
            both[...] = more if f == 0 and k == 0 else both[...] + more

    def activate():
        gate, up = both[:, :HID], both[:, HID:]
        hidden[...] = (gate / (1.0 + jnp.exp(-gate)) * up).astype(jnp.bfloat16)

    def down(f):
        at = lanes(f)

        @pl.loop(0, 4)
        def step(k):
            row = pl.multiple_of(k * QF + STARTS[f], 128)
            part[lax.rem(k, 2), lax.div(k, 2), :, at] = lax.dot_general(
                hidden[...],
                wd[pl.ds(row, WIDTHS[f]), :],
                (((1,), (1,)), ((), ())),
                preferred_element_type=jnp.float32,
            ).astype(jnp.bfloat16)

        copies.start(("mate", f), part.at[1 - c, :, :, at], mate.at[:, :, at], core)

    def chip_sum(f):
        at = lanes(f)
        copies.arrived(("mate", f))
        for h in range(2):
            chip[h, :, at] = (
                part[c, h, :, at].astype(jnp.float32) + mate[h, :, at].astype(jnp.float32)
            ).astype(jnp.bfloat16)
        low, high = pl.ds(0, 128), pl.ds(128, 128)
        copies.start(("r_cross", f), chip.at[1 - yl, high, at], back.at[1, :, at], cross)
        copies.start(("r_far", f), chip.at[yl, high, at], back.at[2, :, at], far)
        copies.start(("r_near", f), chip.at[1 - yl, low, at], back.at[0, :, at], near)

    def expert_out(f):
        at = lanes(f)
        copies.arrived(("r_near", f))
        own = (
            chip[yl, 0:128, at].astype(jnp.float32) + back[0, :, at].astype(jnp.float32)
        ).astype(jnp.bfloat16)
        copies.arrived(("r_cross", f))
        copies.arrived(("r_far", f))
        rest = (
            back[1, :, at].astype(jnp.float32) + back[2, :, at].astype(jnp.float32)
        ).astype(jnp.bfloat16)
        for p in (1, 2, 3, 0):
            into = bbuf if p == 0 else ebuf
            into[p * 64 : p * 64 + 32, at] = own[p * 32 : p * 32 + 32]
            into[p * 64 + 32 : p * 64 + 64, at] = rest[p * 32 : p * 32 + 32]
            if p != 0:
                there = pl.ds(p * 64, 64)
                copies.start(
                    ("r_x", f, p), ebuf.at[there, at], bbuf.at[there, at], at_x(NX - OFFSETS[p])
                )

    def combine(f):
        at = lanes(f)
        for p in (1, 2, 3):
            copies.arrived(("r_x", f, p))
        wide = selw[...]
        high = wide.astype(jnp.bfloat16)
        low = (wide - high.astype(jnp.float32)).astype(jnp.bfloat16)
        contract = (((0,), (0,)), ((), ()))
        joined = bbuf[:, at]
        summed = lax.dot_general(high, joined, contract, preferred_element_type=jnp.float32)
        summed += lax.dot_general(low, joined, contract, preferred_element_type=jnp.float32)
        zsend[:, at] = summed.astype(jnp.bfloat16)
        for d in ALONG_Z:
            there = pl.ds(pl.multiple_of(lax.rem(z + NZ - d, NZ) * ROWS, ROWS), ROWS)
            copies.start(("z", f, d), zsend.at[there, at], zrecv.at[d, :, at], at_z(NZ - d))

    def total(f):
        at = lanes(f)
        out = zsend[own_z, at].astype(jnp.float32)
        for d in ALONG_Z:
            copies.arrived(("z", f, d))
            out += zrecv[d, :, at].astype(jnp.float32)
        moe_ref[:, at] = out.astype(jnp.bfloat16)

    def cache_swap(i):
        own_pieces[i].wait()
        for d in ALONG_Z:
            copies.arrived(("cz", i, d))
        first, second = pl.ds(0, HALF), pl.ds(HALF, HALF)
        copies.start(("swap", i), cz.at[i, first], cz.at[i, second], cross)

    def cache_hot(e):
        lane = iota((HALF, 128), 1).astype(jnp.float32)
        to = lax.rem(x + e, NX)
        for m in range(6):
            line = pos[pl.ds(to * 6 + m, 1), :]
            jb[m * 128 : m * 128 + 128] = jnp.broadcast_to(line, (128, 128)).T
        wants = jnp.concatenate(
            [jb[pl.ds(pl.multiple_of(i * 96 + yh * SLOTS, 16), SLOTS), :] for i in range(NZ)],
            axis=0,
        )
        for k in range(6):
            hots[e, :, k * 128 : k * 128 + 128] = one_hot(wants == lane + 128.0 * k)

    def cache_pick(i):
        copies.arrived(("swap", i))
        for e in (2, 1, 3, 0):
            found = dot(hots[e], cz[i]).astype(jnp.bfloat16)
            if e == 0:
                cxr[0, i] = found
            else:
                cxs[e, i] = found
                copies.start(("cx", i, e), cxs.at[e, i], cxr.at[e, i], at_x(e))

    def own_slots(i, d):
        start = pl.multiple_of(lax.rem(z + d, NZ) * SLOTS, 16)
        return cm.at[i, pl.ds(start, SLOTS)]

    def landing(i):
        lane = pl.multiple_of(lax.rem(z, 2) * 128 + i * 256, 128)
        return keys.at[group, c, lax.div(z, 2), :, pl.ds(lane, 128)]

    own_keys = {}

    def cache_merge(i):
        for e in (1, 3, 2):
            copies.arrived(("cx", i, e))
        cm[i] = (cxr[0, i] + cxr[1, i]) + (cxr[2, i] + cxr[3, i])
        own_keys[i] = pltpu.make_async_copy(
            own_slots(i, 0), landing(i), local_sem.at[2 + PIECES + i]
        )
        own_keys[i].start()
        for d in ALONG_Z:
            copies.start(("k", i, d), own_slots(i, d), landing(i), at_z(d))

    def key_lanes(i):
        return pl.ds(i * 256, 256) if i + 1 < PIECES else pl.ds(KL - 128, 128)

    def cache_tp(i):
        own_keys[i].wait()
        for d in ALONG_Z:
            copies.arrived(("k", i, d))
        there = keys.at[group, c, :, :, key_lanes(i)]
        copies.start(("k_near", i), there, there, near)
        copies.start(("k_core", i, 0), there, there, core)

    def cache_core(i):
        copies.arrived(("k_near", i))
        there = keys.at[1 - group, c, :, :, key_lanes(i)]
        copies.start(("k_core", i, 1), there, there, core)

    def place_queries():
        qp[...] = jnp.zeros_like(qp)
        flat_q = q_ref[...].reshape(256, LAT)
        for i in range(2):
            for h in range(2):
                entry, lane = h * 256 + i * 128, i * 256 + h * 128
                qp[:, lane : lane + 128] = flat_q[:, entry : entry + 128]
        qp[:, 640 : 640 + LAT - KV] = flat_q[:, KV:LAT]

    def attention():
        for i in range(PIECES):
            copies.arrived(("k_core", i, 0))
            copies.arrived(("k_core", i, 1))
        held = keys[...].reshape(TOK, KL)
        rows_with_rows = (((1,), (1,)), ((), ()))
        scores = lax.dot_general(
            qp[:, 0:KV], held[:, 0:KV], rows_with_rows, preferred_element_type=jnp.float32
        )
        scores += lax.dot_general(
            qp[:, KL - 128 : KL],
            held[:, KL - 128 : KL],
            rows_with_rows,
            preferred_element_type=jnp.float32,
        )
        scores *= score_scale
        at = iota((SLOTS, TOK), 1).astype(jnp.float32)
        token = over(at, SLOTS)
        spread = one_hot(at - token * SLOTS == iota((SLOTS, TOK), 0).astype(jnp.float32))
        numbers = jnp.concatenate(
            [
                jnp.broadcast_to(request_ref[...].astype(jnp.float32), (8, SLOTS)),
                jnp.broadcast_to(used_ref[...].astype(jnp.float32), (8, SLOTS)),
            ],
            axis=0,
        ).astype(jnp.bfloat16)
        told = dot(numbers, spread)
        request, used = told[0:1], told[8:9]
        request = jnp.where(token[0:1] < used, request, -1.0)
        row = lax.shift_right_logical(iota((256, TOK), 0), 4).astype(jnp.float32)
        scores = jnp.where(row == request, scores, -1e30)
        terms = jnp.exp(scores - jnp.max(scores, axis=1, keepdims=True))
        weights = (terms / jnp.sum(terms, axis=1, keepdims=True)).astype(jnp.bfloat16)
        attended = dot(weights, held[:, 0:KV]).astype(jnp.bfloat16)
        for i in range(2):
            for h in range(2):
                entry, lane = h * 256 + i * 128, i * 256 + h * 128
                att_ref[:, entry : entry + 128] = attended[:, lane : lane + 128]

    from_z(0)
    cache_hot(2)
    cache_hot(1)
    raw_copy.wait()
    from_x(0)
    from_z(1)
    cache_hot(3)
    cache_swap(0)
    cache_hot(0)
    from_x(1)
    cache_swap(1)
    relay(0)
    from_z(2)
    cache_swap(2)
    lay_out(0, 8)
    from_x(2)
    relay(1)
    lay_out(8, 12)
    from_y(0)
    cache_pick(0)
    cache_pick(1)
    lay_out(12, 22)
    from_y(1)
    cache_pick(2)
    lay_out(22, 28)
    gate_up(0)
    gate_up(1)
    from_y(2)
    wd_copy.wait()
    place_queries()
    gate_up(2)
    activate()
    down(2)
    chip_sum(2)
    down(1)
    chip_sum(1)
    down(0)
    chip_sum(0)
    cache_merge(0)
    cache_merge(1)
    cache_merge(2)
    expert_out(2)
    expert_out(1)
    combine(2)
    cache_tp(0)
    expert_out(0)
    cache_tp(1)
    combine(1)
    cache_tp(2)
    cache_core(0)
    combine(0)
    cache_core(1)
    cache_core(2)
    attention()
    total(2)
    total(1)
    total(0)
    copies.finish()


def hand_out(moe_ref, att_ref, moe_out, att_out):
    moe_out[...] = moe_ref[...]
    att_out[...] = att_ref[...]


def body(
    tokens,
    expert_ids,
    gate_weights,
    expert_gate_up,
    expert_down,
    queries,
    latent_cache,
    block_source,
    block_request,
    block_used,
):
    bf16, f32 = jnp.bfloat16, jnp.float32
    vmem = pl.BlockSpec(memory_space=pltpu.VMEM)
    anyspace = pl.BlockSpec(memory_space=pl.ANY)
    count = 7 + 3 * 37 + 63
    results = (
        jax.ShapeDtypeStruct((ROWS, QF), bf16),
        jax.ShapeDtypeStruct((256, KV), bf16),
    )
    moe, attended = pl.pallas_call(
        kernel,
        out_shape=results,
        in_specs=[vmem] * 8 + [anyspace] * 2,
        out_specs=(vmem, vmem),
        scratch_shapes=[
            pltpu.SemaphoreType.DMA((count,)),
            pltpu.SemaphoreType.DMA((count,)),
            pltpu.SemaphoreType.DMA((8,)),
            pltpu.VMEM((D, 2, HID), bf16),
            pltpu.VMEM((D, 2 * HID), bf16),
            pltpu.VMEM((D, HID), bf16),
            pltpu.VMEM((2 * CHUNK, 2 * CHUNK), bf16),
            pltpu.VMEM((16, 128), f32),
            pltpu.VMEM((NZ, 16, 128), f32),
            pltpu.VMEM((NZ * ROWS, QF), bf16),
            pltpu.VMEM((256, 128), bf16),
            pltpu.VMEM((256, 128), f32),
            pltpu.VMEM((256, QF), bf16),
            pltpu.VMEM((4, 256, QF), bf16),
            pltpu.VMEM((128, QF), bf16),
            pltpu.VMEM((256, 2 * HID), f32),
            pltpu.VMEM((256, HID), bf16),
            pltpu.VMEM((2, 2, 256, QF), bf16),
            pltpu.VMEM((2, 256, QF), bf16),
            pltpu.VMEM((2, 256, QF), bf16),
            pltpu.VMEM((3, 128, QF), bf16),
            pltpu.VMEM((256, QF), bf16),
            pltpu.VMEM((256, QF), bf16),
            pltpu.VMEM((NZ * ROWS, QF), bf16),
            pltpu.VMEM((NZ, ROWS, QF), bf16),
            pltpu.VMEM((4, SLOTS, 640), bf16),
            pltpu.VMEM((24, 128), f32),
            pltpu.VMEM((TOK, 128), f32),
            pltpu.VMEM((PIECES, 2 * HALF, 128), bf16),
            pltpu.VMEM((NX, HALF, 2 * HALF), bf16),
            pltpu.VMEM((NX, PIECES, HALF, 128), bf16),
            pltpu.VMEM((NX, PIECES, HALF, 128), bf16),
            pltpu.VMEM((PIECES, HALF, 128), bf16),
            pltpu.VMEM((2, 2, 4, SLOTS, KL), bf16),
            pltpu.VMEM((256, KL), bf16),
        ],
        compiler_params=pltpu.CompilerParams(
            collective_id=0, has_side_effects=True, vmem_limit_bytes=56 * 2**20
        ),
        cost_estimate=pl.CostEstimate(
            flops=8 * 10**9, bytes_accessed=13 * 10**6, transcendentals=3 * 10**5
        ),
        name="layer",
    )(
        expert_ids.T,
        gate_weights.T,
        tokens,
        latent_cache,
        block_source.reshape(24, 128),
        queries,
        block_request.reshape(1, SLOTS),
        block_used.reshape(1, SLOTS),
        expert_gate_up[0],
        expert_down[0],
    )
    moe, attended = pl.pallas_call(
        hand_out, out_shape=results, in_specs=[vmem] * 2, out_specs=(vmem, vmem), name="results"
    )(moe, attended)
    return moe, attended.reshape(ROWS, 16, KV)


def solution(mesh):
    placed = (
        P("ep", "tp"),
        P("ep", None),
        P("ep", None),
        P("ep", None, None, "tp"),
        P("ep", None, "tp"),
        P("ep", "tp", None),
        P("ep", None, None),
        P(),
        P("ep"),
        P("ep"),
    )
    return jax.shard_map(
        body,
        mesh=mesh,
        in_specs=placed,
        out_specs=(P("ep", "tp"), P("ep", "tp", None)),
        check_vma=False,
    )
```
